256 devices in a mesh: row: 32 (over x, z_lo, y), col: 8 (over z_hi, core).
Axes of the slice: x: 4, y: 4, z: 8 (z_hi: 4, z_lo: 2; z = z_hi * 2 + z_lo), core: 2. Of those that a mesh axis runs over, the one named last changes fastest.
Arguments:
- object_field: float32 [2, 16384, 4096], P(None, 'row', 'col'), may hold values from -13 to 13
- probe_modes: float32 [2, 2, 256, 256], replicated, may hold values from -5 to 5
- scan_offsets: int32 [32, 8, 2, 6], P('row', 'col'), may hold values from 0 to 16128, as said below
- scan_counts: int32 [32, 8], P('row', 'col'), may hold values from 1 to 6, as said below
- amplitudes: bfloat16 [32, 8, 6, 256, 256], P('row', 'col'), may hold values from 0 to 2.5
Outputs:
- object_new: float32 [2, 16384, 4096], P(None, 'row', 'col')
- probe_new: float32 [2, 2, 256, 256], replicated
The draws below stay inside these ranges and needn't reach their ends.
Inputs may be any that keep to these rules, and one draw needn't show every extreme that they name: `scan_counts`: some tile has exactly 6 live positions. `scan_offsets`: each patch of 256 x 256 pixels lies inside the object, and its centre (top-left plus 256 // 2 in each direction) lies in the slot's own tile.
All inputs are finite; a program needn't handle non-finite values.
Results may differ from the reference program's by a relative error of at most 0.0003.
Values sent between devices are 32-bit elements; how exact they have to be, the bound alone decides.
A program may use at most 64 MiB of HBM per device.

```python
import jax
import jax.numpy as jnp
from jax import lax

PROBE = 256
MODES = 2
TILE_H = 512
TILE_W = 512
SLOTS = 6
TILES_R = 32
TILES_C = 8
HEIGHT = 16384
WIDTH = 4096


def scan_plan(key):
    base_key = jax.random.fold_in(key, 7)
    key_list = jax.random.split(base_key, 4)
    tile_count = TILES_R * TILES_C
    rank_draw = jax.random.randint(key_list[0], (tile_count,), 0, SLOTS)
    live_counts = 1 + rank_draw * rank_draw // SLOTS
    busiest = jax.random.randint(key_list[1], (), 0, tile_count)
    live_counts = jnp.where(jnp.arange(tile_count) == busiest, SLOTS, live_counts)
    live_counts = live_counts.astype(jnp.int32).reshape(TILES_R, TILES_C)
    centre_rows = jnp.arange(TILES_R, dtype=jnp.int32)[:, None, None] * TILE_H + jax.random.randint(key_list[2], (TILES_R, TILES_C, SLOTS), 0, TILE_H)
    centre_cols = jnp.arange(TILES_C, dtype=jnp.int32)[None, :, None] * TILE_W + jax.random.randint(key_list[3], (TILES_R, TILES_C, SLOTS), 0, TILE_W)
    top_edge = jnp.clip(centre_rows - PROBE // 2, 0, HEIGHT - PROBE)
    left_edge = jnp.clip(centre_cols - PROBE // 2, 0, WIDTH - PROBE)
    offsets = jnp.stack([top_edge, left_edge], axis=2).astype(jnp.int32)
    return (offsets, live_counts)


def draw_scan_offsets(key, part):
    return scan_plan(key)[0]


def draw_scan_counts(key, part):
    return scan_plan(key)[1]


def draw_object_field(key, part):
    key_list = jax.random.split(jax.random.fold_in(key, 11), 2)
    row_place = jnp.arange(HEIGHT, dtype=jnp.float32) / HEIGHT
    entries = jax.random.truncated_normal(key_list[0], -4.0, 4.0, (2, HEIGHT, WIDTH), jnp.float32)
    row_scale = 10.0 ** (0.5 * row_place - 0.25)
    col_scale = 10.0 ** (0.5 * jax.random.uniform(key_list[1], (WIDTH,), jnp.float32) - 0.25)
    return entries * row_scale[None, :, None] * col_scale[None, None, :]


def levels(stream_key, shape, cuts, low, high):
    def one(dim, shards_of):
        draws = jax.random.uniform(jax.random.fold_in(jax.random.fold_in(stream_key, 6), dim), (shards_of,), jnp.float32, low / len(cuts), high / len(cuts))
        return jnp.repeat(jnp.exp(draws), shape[dim] // shards_of).reshape((-1,) + (1,) * (len(shape) - dim - 1))

    loudness = one(*cuts[0])
    for cut in cuts[1:]:
        loudness = loudness * one(*cut)
    return loudness


def noise(key, dims, width, reach, kind=jnp.bfloat16):
    return jnp.clip(width * jax.random.normal(key, dims, jnp.float32), -reach, reach).astype(kind)


def setup_inputs(seed: int = 0) -> dict:
    arg_keys = jax.random.split(jax.random.key(seed), 6)
    object_field = draw_object_field(jax.random.fold_in(arg_keys[5], 71), 0)
    probe_modes = noise(arg_keys[1], (2, MODES, PROBE, PROBE), 1.0, 5.0, jnp.float32)
    scan_offsets = draw_scan_offsets(jax.random.fold_in(arg_keys[5], 71), 0)
    scan_counts = draw_scan_counts(jax.random.fold_in(arg_keys[5], 71), 0)
    amplitudes = jnp.clip(2.5 * jax.random.uniform(arg_keys[4], (TILES_R, TILES_C, SLOTS, PROBE, PROBE), jnp.float32) ** levels(arg_keys[4], (TILES_R, TILES_C, SLOTS, PROBE, PROBE), ((0, 32), (1, 8)), -0.2, 0.2), 0.0, 2.5).astype(jnp.bfloat16)
    return {"object_field": object_field, "probe_modes": probe_modes, "scan_offsets": scan_offsets, "scan_counts": scan_counts, "amplitudes": amplitudes}


def reference(object_field, probe_modes, scan_offsets, scan_counts, amplitudes):
    float_type = object_field.dtype
    object_complex = lax.complex(object_field[0], object_field[1])
    probe_complex = lax.complex(probe_modes[0], probe_modes[1])
    probe_power = lax.optimization_barrier(jnp.sum(probe_modes[0] * probe_modes[0] + probe_modes[1] * probe_modes[1], axis=0))
    slot_total = TILES_R * TILES_C * SLOTS
    offset_rows = jnp.transpose(scan_offsets, (0, 1, 3, 2)).reshape(slot_total, 2)
    live_flags = (jnp.arange(SLOTS, dtype=jnp.int32)[None, None, :] < scan_counts[:, :, None]).reshape(slot_total)
    amplitude_rows = amplitudes.reshape(slot_total, PROBE, PROBE)

    def visit_slot(position, state_tuple):
        object_grad, lighting, probe_grad, probe_norm = state_tuple
        row_start = offset_rows[position, 0]
        col_start = offset_rows[position, 1]
        weight_live = live_flags[position].astype(float_type)
        patch_field = lax.dynamic_slice(object_complex, (row_start, col_start), (PROBE, PROBE))
        far_field = jnp.fft.fft2(probe_complex * patch_field[None], norm='ortho')
        intensity = lax.optimization_barrier(jnp.sum(far_field.real * far_field.real + far_field.imag * far_field.imag, axis=0))
        factor = amplitude_rows[position].astype(float_type) / jnp.sqrt(jnp.maximum(intensity, 0.25)) - 1.0
        back_field = jnp.fft.ifft2(far_field * factor[None], norm='ortho')
        update = lax.optimization_barrier(jnp.sum(jnp.conj(probe_complex) * back_field, axis=0)) * weight_live
        window = lax.dynamic_slice(object_grad, (row_start, col_start), (PROBE, PROBE))
        object_grad = lax.dynamic_update_slice(object_grad, window + update, (row_start, col_start))
        shade = lax.dynamic_slice(lighting, (row_start, col_start), (PROBE, PROBE))
        lighting = lax.dynamic_update_slice(lighting, shade + probe_power * weight_live, (row_start, col_start))
        probe_grad = probe_grad + jnp.conj(patch_field)[None] * back_field * weight_live
        probe_norm = probe_norm + (patch_field.real * patch_field.real + patch_field.imag * patch_field.imag) * weight_live
        return (object_grad, lighting, probe_grad, probe_norm)
    initial = (jnp.zeros_like(object_complex), jnp.zeros((HEIGHT, WIDTH), float_type), jnp.zeros_like(probe_complex), jnp.zeros((PROBE, PROBE), float_type))
    object_grad, lighting, probe_grad, probe_norm = lax.fori_loop(0, slot_total, visit_slot, initial)
    object_next = object_complex + object_grad / (lighting + 1.0)
    probe_next = probe_complex + probe_grad / (probe_norm + 1.0)[None]
    return (jnp.stack([object_next.real, object_next.imag]), jnp.stack([probe_next.real, probe_next.imag]))
```

```python
import functools
import math

import jax
import jax.numpy as jnp
import numpy as np
from jax import lax
from jax.experimental import pallas as pl
from jax.experimental.pallas import tpu as pltpu
from jax.sharding import PartitionSpec as P

MESH = pl.DeviceIdType.MESH
EDGE = 256
HALF = 128
TILE = 512
MARGIN = 128
EXT = TILE + 2 * MARGIN
SLOTS = 6
SIDES = tuple((dr, dc) for dr in (-1, 0, 1) for dc in (-1, 0, 1))
NEIGHBOURS = ((0, 1), (0, -1), (1, 1), (1, -1), (-1, 1), (-1, -1), (1, 0), (-1, 0))
LIT = 1024
LIT_PAD = LIT + 128
ROWS = 32


def shifted(dr, dc):
    rows, cols = lax.axis_size("row"), lax.axis_size("col")
    row = lax.rem(lax.axis_index("row") + dr + rows, rows)
    col = lax.rem(lax.axis_index("col") + dc + cols, cols)
    return (row, col)


def edge_span(step):
    if step == 0:
        return pl.ds(0, TILE), pl.ds(MARGIN, TILE)
    if step > 0:
        return pl.ds(TILE - MARGIN, MARGIN), pl.ds(0, MARGIN)
    return pl.ds(0, MARGIN), pl.ds(MARGIN + TILE, MARGIN)


def halo_kernel(field, meta, framed, metas, local_sems, send_sems, recv_sems, meta_send, meta_recv):
    barrier = pltpu.get_barrier_semaphore()
    for dr, dc in NEIGHBOURS:
        pl.semaphore_signal(barrier, inc=1, device_id=shifted(dr, dc), device_id_type=MESH)
    own = pltpu.make_async_copy(
        field, framed.at[:, pl.ds(MARGIN, TILE), pl.ds(MARGIN, TILE)], local_sems.at[0]
    )
    own_meta = pltpu.make_async_copy(meta, metas.at[4], local_sems.at[1])
    pl.semaphore_wait(barrier, len(NEIGHBOURS))
    copies = []
    for n, (dr, dc) in enumerate(NEIGHBOURS):
        src_r, dst_r = edge_span(dr)
        src_c, dst_c = edge_span(dc)
        copies.append(
            pltpu.make_async_remote_copy(
                src_ref=field.at[:, src_r, src_c],
                dst_ref=framed.at[:, dst_r, dst_c],
                send_sem=send_sems.at[n],
                recv_sem=recv_sems.at[n],
                device_id=shifted(dr, dc),
                device_id_type=MESH,
            )
        )
        copies.append(
            pltpu.make_async_remote_copy(
                src_ref=meta,
                dst_ref=metas.at[SIDES.index((-dr, -dc))],
                send_sem=meta_send.at[n],
                recv_sem=meta_recv.at[n],
                device_id=shifted(dr, dc),
                device_id_type=MESH,
            )
        )
    for copy in copies:
        copy.start()
    own.start()
    own_meta.start()
    own.wait()
    own_meta.wait()
    for copy in copies:
        copy.wait()


def gather_frame(field, meta):
    any_spec = pl.BlockSpec(memory_space=pl.ANY)
    count = len(NEIGHBOURS)
    return pl.pallas_call(
        halo_kernel,
        out_shape=(
            jax.ShapeDtypeStruct((2, EXT, EXT), jnp.float32),
            jax.ShapeDtypeStruct((9, 8, 128), jnp.int32),
        ),
        in_specs=[any_spec, any_spec],
        out_specs=(any_spec, any_spec),
        scratch_shapes=[
            pltpu.SemaphoreType.DMA((2,)),
            pltpu.SemaphoreType.DMA((count,)),
            pltpu.SemaphoreType.DMA((count,)),
            pltpu.SemaphoreType.DMA((count,)),
            pltpu.SemaphoreType.DMA((count,)),
        ],
        compiler_params=pltpu.CompilerParams(
            collective_id=0, has_side_effects=True, vmem_limit_bytes=4 * 1024 * 1024
        ),
        name="halo",
    )(field, meta)


def split(x):
    high = x.astype(jnp.bfloat16)
    return high, (x - high.astype(jnp.float32)).astype(jnp.bfloat16)


def tables():
    n = np.arange(HALF)
    angle = 2.0 * np.pi * ((n[:, None] * n[None, :]) % HALF) / HALF
    cosine, sine = np.cos(angle), np.sin(angle)
    right = np.block([[cosine, -sine], [sine, cosine]]).astype(np.float32)
    half_angle = 2.0 * np.pi * n / EDGE
    twist = np.stack([np.cos(half_angle), np.sin(half_angle)]).astype(np.float32)
    lanes = np.broadcast_to(twist[:, None, :], (2, 8, HALF))
    subs = np.broadcast_to(twist[:, :, None], (2, HALF, HALF))
    order = np.concatenate([np.arange(0, EDGE, 2), np.arange(1, EDGE, 2)])
    pick = (order[:, None] == np.arange(EDGE)[None, :]).astype(np.float32)
    out = []
    for table in (right, right.T):
        high = table.astype(jnp.bfloat16)
        out += [high, (table - high.astype(np.float32)).astype(jnp.bfloat16)]
    out += [pick.astype(jnp.bfloat16), pick.T.astype(jnp.bfloat16), lanes.copy(), subs.copy()]
    return [jnp.asarray(t) for t in out]


def cat(parts, axis):
    return jnp.concatenate(parts, axis=axis)


def tile_kernel(
    place, metas, framed, probe, amps, rh, rl, lh, ll, pick, pick_t, lane_tw, sub_tw,
    grad, shade, sums,
    patch, xh, xl, yh, yl, amp, light, power,
):
    f32, bf16 = jnp.float32, jnp.bfloat16
    dot = functools.partial(jnp.dot, preferred_element_type=f32)
    lane = lax.broadcasted_iota(jnp.int32, (1, HALF), 1)
    top, left = place[0], place[1]

    grad[...] = jnp.zeros_like(grad)
    sums[...] = jnp.zeros_like(sums)
    for i in range(0, EDGE, ROWS):
        s = pl.ds(i, ROWS)
        power[s, :] = sum(probe[c, k, s, :] * probe[c, k, s, :] for k in range(2) for c in range(2))
    light[pl.ds(256, TILE), pl.ds(256, TILE)] = jnp.zeros((TILE, TILE), f32)

    def spread(low, high, down, shift):
        below = jnp.zeros((8, HALF), f32)
        low, high = (
            pltpu.roll(pltpu.roll(cat([v, below], 0), down, 0), shift, 1) for v in (low, high)
        )
        keep = lane >= shift
        return (
            jnp.where(keep, low, 0.0),
            jnp.where(keep, high, low),
            jnp.where(keep, 0.0, high),
        )

    def light_slot(which, position):
        r = metas[which, 0, position] - top + 256
        c = metas[which, 0, SLOTS + position] - left + 256

        @pl.when((r > 0) & (r < 768) & (c > 0) & (c < 768))
        def _():
            shift, down = lax.rem(c, HALF), lax.rem(r, 8)
            base = pl.multiple_of(c - shift, HALF)
            first = pl.multiple_of(r - down, 8)
            for i in range(0, EDGE, ROWS):
                s = pl.ds(i, ROWS)
                blocks = spread(power[s, :HALF], power[s, HALF:], down, shift)
                for b, block in enumerate(blocks):
                    at = (pl.ds(first + i, ROWS + 8), pl.ds(base + b * HALF, HALF))
                    light[at] += block

    def light_tile(which, _):
        def one(position, _):
            light_slot(which, position)
            return 0

        lax.fori_loop(0, metas[which, 0, 2 * SLOTS], one, 0)
        return 0

    lax.fori_loop(0, 9, light_tile, 0)
    for i in range(0, TILE, ROWS):
        shade[pl.ds(i, ROWS), :] = 1.0 / (light[pl.ds(256 + i, ROWS), pl.ds(256, TILE)] + 1.0)

    right_hhl = cat([rh[...], rh[...], rl[...]], 0)

    def visit(position, _):
        r = metas[4, 0, position] - top + MARGIN
        c = metas[4, 0, SLOTS + position] - left + MARGIN
        shift = lax.rem(c, HALF)
        base = pl.multiple_of(c - shift, HALF)
        down = lax.rem(r, 8)
        first = pl.multiple_of(r - down, 8)
        up = lax.rem(ROWS + 8 - down, ROWS + 8)
        back_shift = lax.rem(HALF - shift, HALF)
        keep = lane < HALF - shift
        picked = dot(pick[...], amps[position]).astype(bf16)
        amp[...] = dot(picked, pick_t[...])

        for i in range(0, EDGE, ROWS):
            s = pl.ds(i, ROWS)
            planes = []
            for plane in range(2):
                rolled = [
                    pltpu.roll(
                        pltpu.roll(
                            framed[
                                plane, pl.ds(first + i, ROWS + 8), pl.ds(base + b * HALF, HALF)
                            ],
                            up,
                            0,
                        )[:ROWS],
                        back_shift,
                        1,
                    )
                    for b in range(3)
                ]
                planes.append(
                    (jnp.where(keep, rolled[0], rolled[1]), jnp.where(keep, rolled[1], rolled[2]))
                )
            for plane in range(2):
                for h in range(2):
                    patch[plane, s, pl.ds(h * HALF, HALF)] = planes[plane][h]
            for k in range(2):
                wr, wi = [], []
                for h in range(2):
                    pr, pi = (probe[p, k, s, pl.ds(h * HALF, HALF)] for p in range(2))
                    wr.append(pr * planes[0][h] - pi * planes[1][h])
                    wi.append(pr * planes[1][h] + pi * planes[0][h])
                cosine, sine = lane_tw[0, :1, :], lane_tw[1, :1, :]
                dr, di = wr[0] - wr[1], wi[0] - wi[1]
                for part, value in (
                    (0, cat([wr[0] + wr[1], wi[0] + wi[1]], 1)),
                    (1, cat([dr * cosine + di * sine, di * cosine - dr * sine], 1)),
                ):
                    high, low = split(value)
                    at = pl.ds((2 * k + part) * EDGE + i, ROWS)
                    xh[at, :] = high
                    xl[at, :] = low

        for k in range(2):
            for i in range(0, HALF, ROWS):
                res = []
                for row in (i, HALF + i):
                    parts = []
                    for part in range(2):
                        at = pl.ds((2 * k + part) * EDGE + row, ROWS)
                        parts.append(dot(cat([xh[at, :], xl[at, :], xh[at, :]], 1), right_hhl))
                    res.append(
                        (
                            cat([parts[0][:, :HALF], parts[1][:, :HALF]], 1),
                            cat([parts[0][:, HALF:], parts[1][:, HALF:]], 1),
                        )
                    )
                (tr, ti), (br, bi) = res
                cosine = cat([sub_tw[0, pl.ds(i, ROWS), :]] * 2, 1)
                sine = cat([sub_tw[1, pl.ds(i, ROWS), :]] * 2, 1)
                dr, di = tr - br, ti - bi
                for part, real, imag in (
                    (0, tr + br, ti + bi),
                    (1, dr * cosine + di * sine, di * cosine - dr * sine),
                ):
                    for start, value in ((0, real), (HALF, imag)):
                        high, low = split(value)
                        at = (2 * k + part, pl.ds(start + i, ROWS), slice(None))
                        yh[at] = high
                        yl[at] = low

        for part in range(2):
            far = [
                dot(
                    cat([lh[...], lh[...], ll[...]], 1),
                    cat([yh[2 * k + part], yl[2 * k + part], yh[2 * k + part]], 0),
                )
                for k in range(2)
            ]
            for i in range(0, HALF, ROWS):
                pieces = [(f[i : i + ROWS], f[HALF + i : HALF + i + ROWS]) for f in far]
                total = sum(a * a + b * b for a, b in pieces)
                total = jnp.maximum(total * (1.0 / 65536.0), 0.25)
                factor = amp[pl.ds(part * HALF + i, ROWS), :] * lax.rsqrt(total) - 1.0
                factor = factor * (1.0 / 65536.0)
                for k in range(2):
                    for start, value in ((0, pieces[k][0]), (HALF, pieces[k][1])):
                        high, low = split(value * factor)
                        at = (2 * k + part, pl.ds(start + i, ROWS), slice(None))
                        yh[at] = high
                        yl[at] = low
        for k in range(2):
            near = [
                dot(
                    cat([rh[...], rh[...], rl[...]], 1),
                    cat([yh[2 * k + part], yl[2 * k + part], yh[2 * k + part]], 0),
                )
                for part in range(2)
            ]
            for i in range(0, HALF, ROWS):
                (ar, ai), (br, bi) = ((f[i : i + ROWS], f[HALF + i : HALF + i + ROWS]) for f in near)
                cosine = cat([sub_tw[0, pl.ds(i, ROWS), :]] * 2, 1)
                sine = cat([sub_tw[1, pl.ds(i, ROWS), :]] * 2, 1)
                br, bi = br * cosine - bi * sine, bi * cosine + br * sine
                for row, real, imag in ((i, ar + br, ai + bi), (HALF + i, ar - br, ai - bi)):
                    for part in range(2):
                        cols = slice(part * HALF, (part + 1) * HALF)
                        high, low = split(cat([real[:, cols], imag[:, cols]], 1))
                        at = pl.ds((2 * k + part) * EDGE + row, ROWS)
                        xh[at, :] = high
                        xl[at, :] = low

        left_hhl = cat([lh[...], lh[...], ll[...]], 0)
        for i in range(0, EDGE, ROWS):
            s = pl.ds(i, ROWS)
            update = [[0.0, 0.0], [0.0, 0.0]]
            cosine, sine = lane_tw[0, :1, :], lane_tw[1, :1, :]
            for k in range(2):
                parts = []
                for part in range(2):
                    at = pl.ds((2 * k + part) * EDGE + i, ROWS)
                    parts.append(dot(cat([xh[at, :], xl[at, :], xh[at, :]], 1), left_hhl))
                ar, ai = parts[0][:, :HALF], parts[0][:, HALF:]
                br, bi = parts[1][:, :HALF], parts[1][:, HALF:]
                br, bi = br * cosine - bi * sine, bi * cosine + br * sine
                for h, real, imag in ((0, ar + br, ai + bi), (1, ar - br, ai - bi)):
                    cols = pl.ds(h * HALF, HALF)
                    pr, pi = probe[0, k, s, cols], probe[1, k, s, cols]
                    update[0][h] += pr * real + pi * imag
                    update[1][h] += pr * imag - pi * real
                    vr, vi = patch[0, s, cols], patch[1, s, cols]
                    sums[k, s, cols] += vr * real + vi * imag
                    sums[2 + k, s, cols] += vr * imag - vi * real
                    if k == 0:
                        sums[4, s, cols] += vr * vr + vi * vi
            for plane in range(2):
                for b, block in enumerate(spread(*update[plane], down, shift)):
                    at = (plane, pl.ds(first + i, ROWS + 8), pl.ds(base + b * HALF, HALF))
                    grad[at] += block
        return 0

    lax.fori_loop(0, metas[4, 0, 2 * SLOTS], visit, 0)


def tile_terms(place, metas, framed, probe, amps):
    vmem = pl.BlockSpec(memory_space=pltpu.VMEM)
    smem = pl.BlockSpec(memory_space=pltpu.SMEM)
    f32, bf16 = jnp.float32, jnp.bfloat16
    consts = tables()
    return pl.pallas_call(
        tile_kernel,
        out_shape=(
            jax.ShapeDtypeStruct((2, EXT, EXT), f32),
            jax.ShapeDtypeStruct((TILE, TILE), f32),
            jax.ShapeDtypeStruct((5, EDGE, EDGE), f32),
        ),
        in_specs=[smem, smem] + [vmem] * (3 + len(consts)),
        out_specs=(vmem, vmem, vmem),
        scratch_shapes=[
            pltpu.VMEM((2, EDGE, EDGE), f32),
            pltpu.VMEM((4 * EDGE, EDGE), bf16),
            pltpu.VMEM((4 * EDGE, EDGE), bf16),
            pltpu.VMEM((4, EDGE, EDGE), bf16),
            pltpu.VMEM((4, EDGE, EDGE), bf16),
            pltpu.VMEM((EDGE, EDGE), f32),
            pltpu.VMEM((LIT, LIT_PAD), f32),
            pltpu.VMEM((EDGE, EDGE), f32),
        ],
        compiler_params=pltpu.CompilerParams(vmem_limit_bytes=56 * 1024 * 1024),
        name="tile",
    )(place, metas, framed, probe, amps, *consts)


def on_device(field, probe, offsets, counts, amps):
    row, col = lax.axis_index("row"), lax.axis_index("col")
    meta = jnp.concatenate([offsets.reshape(2 * SLOTS), counts.reshape(1)])
    meta = jnp.broadcast_to(jnp.pad(meta, (0, 128 - 2 * SLOTS - 1))[None], (8, 128))
    framed, metas = gather_frame(field, meta)
    place = jnp.stack([row * TILE, col * TILE]).astype(jnp.int32)
    grad, shade, sums = tile_terms(place, metas, framed, probe, amps[0, 0])
    return finish(field, probe, grad, shade, sums)


def finish(field, probe, grad, shade, sums):
    inner = grad
    for axis, dim in (("row", 1), ("col", 2)):
        count = lax.axis_size(axis)
        size = inner.shape[dim]
        head = lax.slice_in_dim(inner, 0, MARGIN, axis=dim)
        tail = lax.slice_in_dim(inner, size - MARGIN, size, axis=dim)
        body = lax.slice_in_dim(inner, MARGIN, size - MARGIN, axis=dim)
        from_prev = lax.ppermute(tail, axis, [(i, (i + 1) % count) for i in range(count)])
        from_next = lax.ppermute(head, axis, [((i + 1) % count, i) for i in range(count)])
        pad = [[0, 0], [0, 0], [0, 0]]
        pad[dim] = [0, TILE - MARGIN]
        low = jnp.pad(from_prev, pad)
        pad[dim] = [TILE - MARGIN, 0]
        inner = body + low + jnp.pad(from_next, pad)
    total = lax.psum(sums, ("row", "col"))
    probe_new = probe + total[:4].reshape(2, 2, EDGE, EDGE) / (total[4] + 1.0)
    return (field + inner * shade[None], probe_new)


def solution(mesh):
    in_specs = (
        P(None, "row", "col"),
        P(),
        P("row", "col", None, None),
        P("row", "col"),
        P("row", "col", None, None, None),
    )
    out_specs = (P(None, "row", "col"), P())
    return jax.shard_map(
        on_device, mesh=mesh, in_specs=in_specs, out_specs=out_specs, check_vma=False
    )
```

```python
import functools
import math

import jax
import jax.numpy as jnp
import numpy as np
from jax import lax
from jax.experimental import pallas as pl
from jax.experimental.pallas import tpu as pltpu
from jax.sharding import PartitionSpec as P

MESH = pl.DeviceIdType.MESH
EDGE = 256
HALF = 128
TILE = 512
MARGIN = 128
EXT = TILE + 2 * MARGIN
SLOTS = 6
SIDES = tuple((dr, dc) for dr in (-1, 0, 1) for dc in (-1, 0, 1))
NEIGHBOURS = ((0, 1), (0, -1), (1, 1), (1, -1), (-1, 1), (-1, -1), (1, 0), (-1, 0))
LIT = 1024
LIT_PAD = LIT + 128
ROWS = 32


def shifted(dr, dc):
    rows, cols = lax.axis_size("row"), lax.axis_size("col")
    row = lax.rem(lax.axis_index("row") + dr + rows, rows)
    col = lax.rem(lax.axis_index("col") + dc + cols, cols)
    return (row, col)


def edge_span(step):
    if step == 0:
        return pl.ds(0, TILE), pl.ds(MARGIN, TILE)
    if step > 0:
        return pl.ds(TILE - MARGIN, MARGIN), pl.ds(0, MARGIN)
    return pl.ds(0, MARGIN), pl.ds(MARGIN + TILE, MARGIN)


def halo_kernel(field, meta, framed, metas, local_sems, send_sems, recv_sems, meta_send, meta_recv):
    barrier = pltpu.get_barrier_semaphore()
    for dr, dc in NEIGHBOURS:
        pl.semaphore_signal(barrier, inc=1, device_id=shifted(dr, dc), device_id_type=MESH)
    own = pltpu.make_async_copy(
        field, framed.at[:, pl.ds(MARGIN, TILE), pl.ds(MARGIN, TILE)], local_sems.at[0]
    )
    own_meta = pltpu.make_async_copy(meta, metas.at[4], local_sems.at[1])
    pl.semaphore_wait(barrier, len(NEIGHBOURS))
    copies = []
    for n, (dr, dc) in enumerate(NEIGHBOURS):
        src_r, dst_r = edge_span(dr)
        src_c, dst_c = edge_span(dc)
        copies.append(
            pltpu.make_async_remote_copy(
                src_ref=field.at[:, src_r, src_c],
                dst_ref=framed.at[:, dst_r, dst_c],
                send_sem=send_sems.at[n],
                recv_sem=recv_sems.at[n],
                device_id=shifted(dr, dc),
                device_id_type=MESH,
            )
        )
        copies.append(
            pltpu.make_async_remote_copy(
                src_ref=meta,
                dst_ref=metas.at[SIDES.index((-dr, -dc))],
                send_sem=meta_send.at[n],
                recv_sem=meta_recv.at[n],
                device_id=shifted(dr, dc),
                device_id_type=MESH,
            )
        )
    for copy in copies:
        copy.start()
    own.start()
    own_meta.start()
    own.wait()
    own_meta.wait()
    for copy in copies:
        copy.wait()


def gather_frame(field, meta):
    any_spec = pl.BlockSpec(memory_space=pl.ANY)
    count = len(NEIGHBOURS)
    return pl.pallas_call(
        halo_kernel,
        out_shape=(
            jax.ShapeDtypeStruct((2, EXT, EXT), jnp.float32),
            jax.ShapeDtypeStruct((9, 8, 128), jnp.int32),
        ),
        in_specs=[any_spec, any_spec],
        out_specs=(any_spec, any_spec),
        scratch_shapes=[
            pltpu.SemaphoreType.DMA((2,)),
            pltpu.SemaphoreType.DMA((count,)),
            pltpu.SemaphoreType.DMA((count,)),
            pltpu.SemaphoreType.DMA((count,)),
            pltpu.SemaphoreType.DMA((count,)),
        ],
        compiler_params=pltpu.CompilerParams(
            collective_id=0, has_side_effects=True, vmem_limit_bytes=4 * 1024 * 1024
        ),
        name="halo",
    )(field, meta)


def split(x):
    high = x.astype(jnp.bfloat16)
    return high, (x - high.astype(jnp.float32)).astype(jnp.bfloat16)


def tables():
    n = np.arange(HALF)
    angle = 2.0 * np.pi * ((n[:, None] * n[None, :]) % HALF) / HALF
    cosine, sine = np.cos(angle), np.sin(angle)
    right = np.block([[cosine, -sine], [sine, cosine]]).astype(np.float32)
    half_angle = 2.0 * np.pi * n / EDGE
    twist = np.stack([np.cos(half_angle), np.sin(half_angle)]).astype(np.float32)
    lanes = np.broadcast_to(twist[:, None, :], (2, 8, HALF))
    subs = np.broadcast_to(twist[:, :, None], (2, HALF, HALF))
    order = np.concatenate([np.arange(0, EDGE, 2), np.arange(1, EDGE, 2)])
    pick = (order[:, None] == np.arange(EDGE)[None, :]).astype(np.float32)
    out = []
    for table in (right, right.T):
        high = table.astype(jnp.bfloat16)
        out += [high, (table - high.astype(np.float32)).astype(jnp.bfloat16)]
    out += [pick.astype(jnp.bfloat16), pick.T.astype(jnp.bfloat16), lanes.copy(), subs.copy()]
    return [jnp.asarray(t) for t in out]


def cat(parts, axis):
    return jnp.concatenate(parts, axis=axis)


def tile_kernel(
    place, metas, framed, probe, amps, rh, rl, lh, ll, pick, pick_t, lane_tw, sub_tw,
    grad, shade, sums,
    patch, xh, xl, yh, yl, amp, light, power,
):
    f32, bf16 = jnp.float32, jnp.bfloat16
    dot = functools.partial(jnp.dot, preferred_element_type=f32)
    lane = lax.broadcasted_iota(jnp.int32, (1, HALF), 1)
    top, left = place[0], place[1]

    grad[...] = jnp.zeros_like(grad)
    sums[...] = jnp.zeros_like(sums)
    for i in range(0, EDGE, ROWS):
        s = pl.ds(i, ROWS)
        power[s, :] = sum(probe[c, k, s, :] * probe[c, k, s, :] for k in range(2) for c in range(2))
    light[pl.ds(256, TILE), pl.ds(256, TILE)] = jnp.zeros((TILE, TILE), f32)

    def spread(low, high, down, shift):
        below = jnp.zeros((8, HALF), f32)
        low, high = (
            pltpu.roll(pltpu.roll(cat([v, below], 0), down, 0), shift, 1) for v in (low, high)
        )
        keep = lane >= shift
        return (
            jnp.where(keep, low, 0.0),
            jnp.where(keep, high, low),
            jnp.where(keep, 0.0, high),
        )

    def light_slot(which, position):
        r = metas[which, 0, position] - top + 256
        c = metas[which, 0, SLOTS + position] - left + 256

        @pl.when((r > 0) & (r < 768) & (c > 0) & (c < 768))
        def _():
            shift, down = lax.rem(c, HALF), lax.rem(r, 8)
            base = pl.multiple_of(c - shift, HALF)
            first = pl.multiple_of(r - down, 8)
            for i in range(0, EDGE, ROWS):
                s = pl.ds(i, ROWS)
                blocks = spread(power[s, :HALF], power[s, HALF:], down, shift)
                for b, block in enumerate(blocks):
                    at = (pl.ds(first + i, ROWS + 8), pl.ds(base + b * HALF, HALF))
                    light[at] += block

    def light_tile(which, _):
        def one(position, _):
            light_slot(which, position)
            return 0

        lax.fori_loop(0, metas[which, 0, 2 * SLOTS], one, 0)
        return 0

    lax.fori_loop(0, 9, light_tile, 0)
    for i in range(0, TILE, ROWS):
        shade[pl.ds(i, ROWS), :] = 1.0 / (light[pl.ds(256 + i, ROWS), pl.ds(256, TILE)] + 1.0)

    right_hhl = cat([rh[...], rh[...], rl[...]], 0)

    def visit(position, _):
        r = metas[4, 0, position] - top + MARGIN
        c = metas[4, 0, SLOTS + position] - left + MARGIN
        shift = lax.rem(c, HALF)
        base = pl.multiple_of(c - shift, HALF)
        down = lax.rem(r, 8)
        first = pl.multiple_of(r - down, 8)
        up = lax.rem(ROWS + 8 - down, ROWS + 8)
        back_shift = lax.rem(HALF - shift, HALF)
        keep = lane < HALF - shift
        picked = dot(pick[...], amps[position]).astype(bf16)
        amp[...] = dot(picked, pick_t[...])

        for i in range(0, EDGE, ROWS):
            s = pl.ds(i, ROWS)
            planes = []
            for plane in range(2):
                rolled = [
                    pltpu.roll(
                        pltpu.roll(
                            framed[
                                plane, pl.ds(first + i, ROWS + 8), pl.ds(base + b * HALF, HALF)
                            ],
                            up,
                            0,
                        )[:ROWS],
                        back_shift,
                        1,
                    )
                    for b in range(3)
                ]
                planes.append(
                    (jnp.where(keep, rolled[0], rolled[1]), jnp.where(keep, rolled[1], rolled[2]))
                )
            for plane in range(2):
                for h in range(2):
                    patch[plane, s, pl.ds(h * HALF, HALF)] = planes[plane][h]
            for k in range(2):
                wr, wi = [], []
                for h in range(2):
                    pr, pi = (probe[p, k, s, pl.ds(h * HALF, HALF)] for p in range(2))
                    wr.append(pr * planes[0][h] - pi * planes[1][h])
                    wi.append(pr * planes[1][h] + pi * planes[0][h])
                cosine, sine = lane_tw[0, :1, :], lane_tw[1, :1, :]
                dr, di = wr[0] - wr[1], wi[0] - wi[1]
                for part, value in (
                    (0, cat([wr[0] + wr[1], wi[0] + wi[1]], 1)),
                    (1, cat([dr * cosine + di * sine, di * cosine - dr * sine], 1)),
                ):
                    high, low = split(value)
                    at = pl.ds((2 * k + part) * EDGE + i, ROWS)
                    xh[at, :] = high
                    xl[at, :] = low

        for k in range(2):
            for i in range(0, HALF, ROWS):
                res = []
                for row in (i, HALF + i):
                    parts = []
                    for part in range(2):
                        at = pl.ds((2 * k + part) * EDGE + row, ROWS)
                        parts.append(dot(cat([xh[at, :], xl[at, :], xh[at, :]], 1), right_hhl))
                    res.append(
                        (
                            cat([parts[0][:, :HALF], parts[1][:, :HALF]], 1),
                            cat([parts[0][:, HALF:], parts[1][:, HALF:]], 1),
                        )
                    )
                (tr, ti), (br, bi) = res
                cosine = cat([sub_tw[0, pl.ds(i, ROWS), :]] * 2, 1)
                sine = cat([sub_tw[1, pl.ds(i, ROWS), :]] * 2, 1)
                dr, di = tr - br, ti - bi
                for part, real, imag in (
                    (0, tr + br, ti + bi),
                    (1, dr * cosine + di * sine, di * cosine - dr * sine),
                ):
                    for start, value in ((0, real), (HALF, imag)):
                        high, low = split(value)
                        at = (2 * k + part, pl.ds(start + i, ROWS), slice(None))
                        yh[at] = high
                        yl[at] = low

        for part in range(2):
            far = [
                dot(
                    cat([lh[...], lh[...], ll[...]], 1),
                    cat([yh[2 * k + part], yl[2 * k + part], yh[2 * k + part]], 0),
                )
                for k in range(2)
            ]
            for i in range(0, HALF, ROWS):
                pieces = [(f[i : i + ROWS], f[HALF + i : HALF + i + ROWS]) for f in far]
                total = sum(a * a + b * b for a, b in pieces)
                total = jnp.maximum(total * (1.0 / 65536.0), 0.25)
                factor = amp[pl.ds(part * HALF + i, ROWS), :] * lax.rsqrt(total) - 1.0
                factor = factor * (1.0 / 65536.0)
                for k in range(2):
                    for start, value in ((0, pieces[k][0]), (HALF, pieces[k][1])):
                        high, low = split(value * factor)
                        at = (2 * k + part, pl.ds(start + i, ROWS), slice(None))
                        yh[at] = high
                        yl[at] = low
        for k in range(2):
            near = [
                dot(
                    cat([rh[...], rh[...], rl[...]], 1),
                    cat([yh[2 * k + part], yl[2 * k + part], yh[2 * k + part]], 0),
                )
                for part in range(2)
            ]
            for i in range(0, HALF, ROWS):
                (ar, ai), (br, bi) = ((f[i : i + ROWS], f[HALF + i : HALF + i + ROWS]) for f in near)
                cosine = cat([sub_tw[0, pl.ds(i, ROWS), :]] * 2, 1)
                sine = cat([sub_tw[1, pl.ds(i, ROWS), :]] * 2, 1)
                br, bi = br * cosine - bi * sine, bi * cosine + br * sine
                for row, real, imag in ((i, ar + br, ai + bi), (HALF + i, ar - br, ai - bi)):
                    for part in range(2):
                        cols = slice(part * HALF, (part + 1) * HALF)
                        high, low = split(cat([real[:, cols], imag[:, cols]], 1))
                        at = pl.ds((2 * k + part) * EDGE + row, ROWS)
                        xh[at, :] = high
                        xl[at, :] = low

        left_hhl = cat([lh[...], lh[...], ll[...]], 0)
        for i in range(0, EDGE, ROWS):
            s = pl.ds(i, ROWS)
            update = [[0.0, 0.0], [0.0, 0.0]]
            cosine, sine = lane_tw[0, :1, :], lane_tw[1, :1, :]
            for k in range(2):
                parts = []
                for part in range(2):
                    at = pl.ds((2 * k + part) * EDGE + i, ROWS)
                    parts.append(dot(cat([xh[at, :], xl[at, :], xh[at, :]], 1), left_hhl))
                ar, ai = parts[0][:, :HALF], parts[0][:, HALF:]
                br, bi = parts[1][:, :HALF], parts[1][:, HALF:]
                br, bi = br * cosine - bi * sine, bi * cosine + br * sine
                for h, real, imag in ((0, ar + br, ai + bi), (1, ar - br, ai - bi)):
                    cols = pl.ds(h * HALF, HALF)
                    pr, pi = probe[0, k, s, cols], probe[1, k, s, cols]
                    update[0][h] += pr * real + pi * imag
                    update[1][h] += pr * imag - pi * real
                    vr, vi = patch[0, s, cols], patch[1, s, cols]
                    sums[k, s, cols] += vr * real + vi * imag
                    sums[2 + k, s, cols] += vr * imag - vi * real
                    if k == 0:
                        sums[4, s, cols] += vr * vr + vi * vi
            for plane in range(2):
                for b, block in enumerate(spread(*update[plane], down, shift)):
                    at = (plane, pl.ds(first + i, ROWS + 8), pl.ds(base + b * HALF, HALF))
                    grad[at] += block
        return 0

    lax.fori_loop(0, metas[4, 0, 2 * SLOTS], visit, 0)


def tile_terms(place, metas, framed, probe, amps):
    vmem = pl.BlockSpec(memory_space=pltpu.VMEM)
    smem = pl.BlockSpec(memory_space=pltpu.SMEM)
    f32, bf16 = jnp.float32, jnp.bfloat16
    consts = tables()
    return pl.pallas_call(
        tile_kernel,
        out_shape=(
            jax.ShapeDtypeStruct((2, EXT, EXT), f32),
            jax.ShapeDtypeStruct((TILE, TILE), f32),
            jax.ShapeDtypeStruct((5, EDGE, EDGE), f32),
        ),
        in_specs=[smem, smem] + [vmem] * (3 + len(consts)),
        out_specs=(vmem, vmem, vmem),
        scratch_shapes=[
            pltpu.VMEM((2, EDGE, EDGE), f32),
            pltpu.VMEM((4 * EDGE, EDGE), bf16),
            pltpu.VMEM((4 * EDGE, EDGE), bf16),
            pltpu.VMEM((4, EDGE, EDGE), bf16),
            pltpu.VMEM((4, EDGE, EDGE), bf16),
            pltpu.VMEM((EDGE, EDGE), f32),
            pltpu.VMEM((LIT, LIT_PAD), f32),
            pltpu.VMEM((EDGE, EDGE), f32),
        ],
        compiler_params=pltpu.CompilerParams(vmem_limit_bytes=56 * 1024 * 1024),
        name="tile",
    )(place, metas, framed, probe, amps, *consts)


RIM_SOURCE = {-1: (0, MARGIN), 0: (MARGIN, TILE), 1: (MARGIN + TILE, MARGIN)}
RIM_TARGET = {1: (0, MARGIN), 0: (0, TILE), -1: (TILE - MARGIN, MARGIN)}


def torus_place():
    row, col = lax.axis_index("row"), lax.axis_index("col")
    return (
        row // 8,
        lax.rem(row, 4),
        (col // 2) * 2 + lax.rem(row // 4, 2),
        lax.rem(col, 2),
    )


def torus_device(x, y, z, core):
    return (x * 8 + lax.rem(z, 2) * 4 + y, (z // 2) * 2 + core)


def fold_kernel(
    grad, field, shade, sums, probe, object_out, probe_out,
    inner, base, lit, rims_r, rims_c, rims_d, pair_in, x_in, y_in, z_in, acc, rows_out, row_new, rows_in, spread,
    local_sems, rim_send, rim_recv, red_send, red_recv, put_send, put_recv,
):
    f32 = jnp.float32
    x, y, z, core = torus_place()
    pair = torus_device(x, y, z, 1 - core)
    x_peers = [torus_device(lax.rem(x + d, 4), y, z, core) for d in range(1, 4)]
    y_peers = [torus_device(x, lax.rem(y + d, 4), z, core) for d in range(1, 4)]
    z_peers = [torus_device(x, y, lax.rem(z + d, 8), core) for d in range(1, 8)]

    def ref_of(n):
        if n < 2:
            return rims_c.at[n]
        if n < 6:
            return rims_d.at[n - 2]
        return rims_r.at[n - 6]

    barrier = pltpu.get_barrier_semaphore()
    partners = [shifted(dr, dc) for dr, dc in NEIGHBOURS] + [pair] + x_peers + y_peers + z_peers
    for device in partners:
        pl.semaphore_signal(barrier, inc=1, device_id=device, device_id_type=MESH)
    locals_ = [
        pltpu.make_async_copy(
            grad.at[:, pl.ds(MARGIN, TILE), pl.ds(MARGIN, TILE)], inner, local_sems.at[0]
        ),
        pltpu.make_async_copy(field, base, local_sems.at[1]),
        pltpu.make_async_copy(shade, lit, local_sems.at[2]),
    ]
    pl.semaphore_wait(barrier, len(partners))

    def send(src, dst, device, sems, n):
        copy = pltpu.make_async_remote_copy(
            src_ref=src,
            dst_ref=dst,
            send_sem=sems[0].at[n],
            recv_sem=sems[1].at[n],
            device_id=device,
            device_id_type=MESH,
        )
        copy.start()
        return copy

    red, put = (red_send, red_recv), (put_send, put_recv)
    half = pl.multiple_of(core * HALF, HALF)
    other = pl.multiple_of((1 - core) * HALF, HALF)
    to_pair = send(sums.at[:, pl.ds(other, HALF), :], pair_in, pair, red, 0)
    rims = []
    for n, (dr, dc) in enumerate(NEIGHBOURS):
        src = grad.at[:, pl.ds(*RIM_SOURCE[dr]), pl.ds(*RIM_SOURCE[dc])]
        rims.append(send(src, ref_of(n), shifted(dr, dc), (rim_send, rim_recv), n))
    for copy in locals_:
        copy.start()

    to_pair.wait()
    for i in range(0, HALF, ROWS):
        rows = pl.ds(i, ROWS)
        acc[:, rows, :] = sums[:, pl.ds(pl.multiple_of(half + i, ROWS), ROWS), :] + pair_in[:, rows, :]
    copies = []
    for d in range(1, 4):
        at = pl.multiple_of(lax.rem(x + d, 4) * 32, 32)
        copies.append(send(acc.at[:, pl.ds(at, 32), :], x_in.at[d - 1], x_peers[d - 1], red, d))
    for copy in copies:
        copy.wait()
    x_at = pl.multiple_of(x * 32, 32)
    mine = acc[:, pl.ds(x_at, 32), :]
    for d in range(3):
        mine = mine + x_in[d]
    acc[:, pl.ds(x_at, 32), :] = mine
    copies = []
    for d in range(1, 4):
        at = pl.multiple_of(x_at + lax.rem(y + d, 4) * 8, 8)
        copies.append(send(acc.at[:, pl.ds(at, 8), :], y_in.at[d - 1], y_peers[d - 1], red, 3 + d))
    for copy in copies:
        copy.wait()
    y_at = pl.multiple_of(x_at + y * 8, 8)
    mine = acc[:, pl.ds(y_at, 8), :]
    for d in range(3):
        mine = mine + y_in[d]
    rows_out[...] = jnp.zeros_like(rows_out)
    for r in range(8):
        for p in range(5):
            rows_out[r, pl.ds(p, 1), :] = mine[p, r : r + 1, :]
    copies = []
    for d in range(1, 8):
        copies.append(send(rows_out.at[lax.rem(z + d, 8)], z_in.at[d - 1], z_peers[d - 1], red, 6 + d))
    for copy in copies:
        copy.wait()
    total = rows_out[z]
    for d in range(7):
        total = total + z_in[d]
    row_new[...] = total / (total[4:5] + 1.0)

    copies = []
    for d in range(1, 8):
        copies.append(send(row_new, rows_in.at[z], z_peers[d - 1], put, d))
    rows_in[z] = row_new[...]
    for copy in copies:
        copy.wait()
    at = pl.multiple_of(half + y_at, 8)
    for p in range(4):
        spread[p, pl.ds(at, 8), :] = jnp.concatenate([rows_in[r, pl.ds(p, 1), :] for r in range(8)], 0)
    copies = []
    block = spread.at[:, pl.ds(at, 8), :]
    for d in range(1, 4):
        copies.append(send(block, block, y_peers[d - 1], put, 7 + d))
    for copy in copies:
        copy.wait()
    block = spread.at[:, pl.ds(pl.multiple_of(half + x_at, 32), 32), :]
    copies = []
    for d in range(1, 4):
        copies.append(send(block, block, x_peers[d - 1], put, 10 + d))
    for copy in copies:
        copy.wait()
    block = spread.at[:, pl.ds(half, HALF), :]
    last = send(block, block, pair, put, 0)

    for copy in locals_:
        copy.wait()
    for n, (dr, dc) in enumerate(NEIGHBOURS):
        rims[n].wait()
        (r0, rn), (c0, cn) = RIM_TARGET[dr], RIM_TARGET[dc]
        for i in range(0, rn, 64):
            inner[:, pl.ds(r0 + i, 64), pl.ds(c0, cn)] += ref_of(n)[:, pl.ds(i, 64), :]
    for i in range(0, TILE, ROWS):
        rows = pl.ds(i, ROWS)
        for c in range(2):
            object_out[c, rows, :] = base[c, rows, :] + inner[c, rows, :] * lit[rows, :]
    last.wait()
    for c in range(2):
        for k in range(2):
            probe_out[c, k] = probe[c, k] + spread[2 * c + k]


def fold(grad, field, shade, sums, probe):
    vmem = pl.BlockSpec(memory_space=pltpu.VMEM)
    any_spec = pl.BlockSpec(memory_space=pl.ANY)
    f32 = jnp.float32
    dma = pltpu.SemaphoreType.DMA
    return pl.pallas_call(
        fold_kernel,
        out_shape=(
            jax.ShapeDtypeStruct((2, TILE, TILE), f32),
            jax.ShapeDtypeStruct((2, 2, EDGE, EDGE), f32),
        ),
        in_specs=[any_spec, any_spec, any_spec, vmem, vmem],
        out_specs=(vmem, vmem),
        scratch_shapes=[
            pltpu.VMEM((2, TILE, TILE), f32),
            pltpu.VMEM((2, TILE, TILE), f32),
            pltpu.VMEM((TILE, TILE), f32),
            pltpu.VMEM((2, 2, MARGIN, TILE), f32),
            pltpu.VMEM((2, 2, TILE, MARGIN), f32),
            pltpu.VMEM((4, 2, MARGIN, MARGIN), f32),
            pltpu.VMEM((5, HALF, EDGE), f32),
            pltpu.VMEM((3, 5, 32, EDGE), f32),
            pltpu.VMEM((3, 5, 8, EDGE), f32),
            pltpu.VMEM((7, 8, EDGE), f32),
            pltpu.VMEM((5, HALF, EDGE), f32),
            pltpu.VMEM((8, 8, EDGE), f32),
            pltpu.VMEM((8, EDGE), f32),
            pltpu.VMEM((8, 8, EDGE), f32),
            pltpu.VMEM((4, EDGE, EDGE), f32),
            dma((3,)), dma((8,)), dma((8,)), dma((14,)), dma((14,)), dma((14,)), dma((14,)),
        ],
        compiler_params=pltpu.CompilerParams(
            collective_id=1, has_side_effects=True, vmem_limit_bytes=40 * 1024 * 1024
        ),
        name="fold",
    )(grad, field, shade, sums, probe)


def on_device(field, probe, offsets, counts, amps):
    row, col = lax.axis_index("row"), lax.axis_index("col")
    meta = jnp.concatenate([offsets.reshape(2 * SLOTS), counts.reshape(1)])
    meta = jnp.broadcast_to(jnp.pad(meta, (0, 128 - 2 * SLOTS - 1))[None], (8, 128))
    framed, metas = gather_frame(field, meta)
    place = jnp.stack([row * TILE, col * TILE]).astype(jnp.int32)
    grad, shade, sums = tile_terms(place, metas, framed, probe, amps[0, 0])
    return fold(grad, field, shade, sums, probe)


def solution(mesh):
    in_specs = (
        P(None, "row", "col"),
        P(),
        P("row", "col", None, None),
        P("row", "col"),
        P("row", "col", None, None, None),
    )
    out_specs = (P(None, "row", "col"), P())
    return jax.shard_map(
        on_device, mesh=mesh, in_specs=in_specs, out_specs=out_specs, check_vma=False
    )
```

```python
import functools
import math

import jax
import jax.numpy as jnp
import numpy as np
from jax import lax
from jax.experimental import pallas as pl
from jax.experimental.pallas import tpu as pltpu
from jax.sharding import PartitionSpec as P

MESH = pl.DeviceIdType.MESH
EDGE = 256
HALF = 128
TILE = 512
MARGIN = 128
EXT = TILE + 2 * MARGIN
SLOTS = 6
SIDES = tuple((dr, dc) for dr in (-1, 0, 1) for dc in (-1, 0, 1))
NEIGHBOURS = ((0, 1), (0, -1), (1, 1), (1, -1), (-1, 1), (-1, -1), (1, 0), (-1, 0))
LIT = 1024
LIT_PAD = LIT + 128
ROWS = 32


def shifted(dr, dc):
    rows, cols = lax.axis_size("row"), lax.axis_size("col")
    row = lax.rem(lax.axis_index("row") + dr + rows, rows)
    col = lax.rem(lax.axis_index("col") + dc + cols, cols)
    return (row, col)


def edge_span(step):
    if step == 0:
        return pl.ds(0, TILE), pl.ds(MARGIN, TILE)
    if step > 0:
        return pl.ds(TILE - MARGIN, MARGIN), pl.ds(0, MARGIN)
    return pl.ds(0, MARGIN), pl.ds(MARGIN + TILE, MARGIN)


def halo_kernel(field, meta, framed, metas, local_sems, send_sems, recv_sems, meta_send, meta_recv):
    barrier = pltpu.get_barrier_semaphore()
    for dr, dc in NEIGHBOURS:
        pl.semaphore_signal(barrier, inc=1, device_id=shifted(dr, dc), device_id_type=MESH)
    own = pltpu.make_async_copy(
        field, framed.at[:, pl.ds(MARGIN, TILE), pl.ds(MARGIN, TILE)], local_sems.at[0]
    )
    own_meta = pltpu.make_async_copy(meta, metas.at[4], local_sems.at[1])
    pl.semaphore_wait(barrier, len(NEIGHBOURS))
    copies = []
    for n, (dr, dc) in enumerate(NEIGHBOURS):
        src_r, dst_r = edge_span(dr)
        src_c, dst_c = edge_span(dc)
        copies.append(
            pltpu.make_async_remote_copy(
                src_ref=field.at[:, src_r, src_c],
                dst_ref=framed.at[:, dst_r, dst_c],
                send_sem=send_sems.at[n],
                recv_sem=recv_sems.at[n],
                device_id=shifted(dr, dc),
                device_id_type=MESH,
            )
        )
        copies.append(
            pltpu.make_async_remote_copy(
                src_ref=meta,
                dst_ref=metas.at[SIDES.index((-dr, -dc))],
                send_sem=meta_send.at[n],
                recv_sem=meta_recv.at[n],
                device_id=shifted(dr, dc),
                device_id_type=MESH,
            )
        )
    for copy in copies:
        copy.start()
    own.start()
    own_meta.start()
    own.wait()
    own_meta.wait()
    for copy in copies:
        copy.wait()


def gather_frame(field, meta):
    any_spec = pl.BlockSpec(memory_space=pl.ANY)
    count = len(NEIGHBOURS)
    vmem = pl.BlockSpec(memory_space=pltpu.VMEM)
    return pl.pallas_call(
        halo_kernel,
        out_shape=(
            jax.ShapeDtypeStruct((2, EXT, EXT), jnp.float32),
            jax.ShapeDtypeStruct((9, 8, 128), jnp.int32),
        ),
        in_specs=[any_spec, any_spec],
        out_specs=(vmem, any_spec),
        scratch_shapes=[
            pltpu.SemaphoreType.DMA((2,)),
            pltpu.SemaphoreType.DMA((count,)),
            pltpu.SemaphoreType.DMA((count,)),
            pltpu.SemaphoreType.DMA((count,)),
            pltpu.SemaphoreType.DMA((count,)),
        ],
        compiler_params=pltpu.CompilerParams(
            collective_id=0, has_side_effects=True, vmem_limit_bytes=16 * 1024 * 1024
        ),
        name="halo",
    )(field, meta)


def split(x):
    high = x.astype(jnp.bfloat16)
    return high, (x - high.astype(jnp.float32)).astype(jnp.bfloat16)


def tables():
    n = np.arange(HALF)
    angle = 2.0 * np.pi * ((n[:, None] * n[None, :]) % HALF) / HALF
    cosine, sine = np.cos(angle), np.sin(angle)
    right = np.block([[cosine, -sine], [sine, cosine]]).astype(np.float32)
    half_angle = 2.0 * np.pi * n / EDGE
    twist = np.stack([np.cos(half_angle), np.sin(half_angle)]).astype(np.float32)
    lanes = np.broadcast_to(twist[:, None, :], (2, 8, HALF))
    subs = np.broadcast_to(twist[:, :, None], (2, HALF, HALF))
    order = np.concatenate([np.arange(0, EDGE, 2), np.arange(1, EDGE, 2)])
    pick = (order[:, None] == np.arange(EDGE)[None, :]).astype(np.float32)
    out = []
    for table in (right, right.T):
        high = table.astype(jnp.bfloat16)
        out += [high, (table - high.astype(np.float32)).astype(jnp.bfloat16)]
    out += [pick.astype(jnp.bfloat16), pick.T.astype(jnp.bfloat16), lanes.copy(), subs.copy()]
    return [jnp.asarray(t) for t in out]


def cat(parts, axis):
    return jnp.concatenate(parts, axis=axis)


def tile_kernel(
    place, metas, framed, probe, amps, rh, rl, lh, ll, pick, pick_t, lane_tw, sub_tw,
    grad, shade, sums,
    patch, xh, xl, yh, yl, amp, light, power, whole,
):
    f32, bf16 = jnp.float32, jnp.bfloat16
    dot = functools.partial(jnp.dot, preferred_element_type=f32)
    lane = lax.broadcasted_iota(jnp.int32, (1, HALF), 1)
    top, left = place[0], place[1]

    grad[...] = jnp.zeros_like(grad)
    sums[...] = jnp.zeros_like(sums)
    for i in range(0, EDGE, ROWS):
        s = pl.ds(i, ROWS)
        power[s, :] = sum(probe[c, k, s, :] * probe[c, k, s, :] for k in range(2) for c in range(2))
    light[pl.ds(256, TILE), pl.ds(256, TILE)] = jnp.zeros((TILE, TILE), f32)

    def spread(low, high, down, shift):
        below = jnp.zeros((8, HALF), f32)
        low, high = (
            pltpu.roll(pltpu.roll(cat([v, below], 0), down, 0), shift, 1) for v in (low, high)
        )
        keep = lane >= shift
        return (
            jnp.where(keep, low, 0.0),
            jnp.where(keep, high, low),
            jnp.where(keep, 0.0, high),
        )

    def light_slot(which, position):
        r = metas[which, 0, position] - top + 256
        c = metas[which, 0, SLOTS + position] - left + 256

        @pl.when((r > 0) & (r < 768) & (c > 0) & (c < 768))
        def _():
            shift, down = lax.rem(c, HALF), lax.rem(r, 8)
            base = pl.multiple_of(c - shift, HALF)
            first = pl.multiple_of(r - down, 8)
            for i in range(0, EDGE, ROWS):
                s = pl.ds(i, ROWS)
                blocks = spread(power[s, :HALF], power[s, HALF:], down, shift)
                for b, block in enumerate(blocks):
                    at = (pl.ds(first + i, ROWS + 8), pl.ds(base + b * HALF, HALF))
                    light[at] += block

    def light_tile(which, _):
        def one(position, _):
            light_slot(which, position)
            return 0

        lax.fori_loop(0, metas[which, 0, 2 * SLOTS], one, 0)
        return 0

    lax.fori_loop(0, 9, light_tile, 0)
    for i in range(0, TILE, ROWS):
        shade[pl.ds(i, ROWS), :] = 1.0 / (light[pl.ds(256 + i, ROWS), pl.ds(256, TILE)] + 1.0)

    right_hhl = cat([rh[...], rh[...], rl[...]], 0)

    def visit(position, _):
        r = metas[4, 0, position] - top + MARGIN
        c = metas[4, 0, SLOTS + position] - left + MARGIN
        shift = lax.rem(c, HALF)
        base = pl.multiple_of(c - shift, HALF)
        down = lax.rem(r, 8)
        first = pl.multiple_of(r - down, 8)
        up = lax.rem(ROWS + 8 - down, ROWS + 8)
        back_shift = lax.rem(HALF - shift, HALF)
        keep = lane < HALF - shift
        picked = dot(pick[...], amps[position]).astype(bf16)
        amp[...] = dot(picked, pick_t[...])

        for i in range(0, EDGE, ROWS):
            s = pl.ds(i, ROWS)
            planes = []
            for plane in range(2):
                rolled = [
                    pltpu.roll(
                        pltpu.roll(
                            framed[
                                plane, pl.ds(first + i, ROWS + 8), pl.ds(base + b * HALF, HALF)
                            ],
                            up,
                            0,
                        )[:ROWS],
                        back_shift,
                        1,
                    )
                    for b in range(3)
                ]
                planes.append(
                    (jnp.where(keep, rolled[0], rolled[1]), jnp.where(keep, rolled[1], rolled[2]))
                )
            for plane in range(2):
                for h in range(2):
                    patch[plane, s, pl.ds(h * HALF, HALF)] = planes[plane][h]
            for k in range(2):
                wr, wi = [], []
                for h in range(2):
                    pr, pi = (probe[p, k, s, pl.ds(h * HALF, HALF)] for p in range(2))
                    wr.append(pr * planes[0][h] - pi * planes[1][h])
                    wi.append(pr * planes[1][h] + pi * planes[0][h])
                cosine, sine = lane_tw[0, :1, :], lane_tw[1, :1, :]
                dr, di = wr[0] - wr[1], wi[0] - wi[1]
                for part, value in (
                    (0, cat([wr[0] + wr[1], wi[0] + wi[1]], 1)),
                    (1, cat([dr * cosine + di * sine, di * cosine - dr * sine], 1)),
                ):
                    high, low = split(value)
                    at = pl.ds((2 * k + part) * EDGE + i, ROWS)
                    xh[at, :] = high
                    xl[at, :] = low

        whole[...] = dot(cat([xh[...], xl[...], xh[...]], 1), right_hhl)
        for k in range(2):
            for i in range(0, HALF, ROWS):
                res = []
                for row in (i, HALF + i):
                    parts = [
                        whole[pl.ds((2 * k + part) * EDGE + row, ROWS), :] for part in range(2)
                    ]
                    res.append(
                        (
                            cat([parts[0][:, :HALF], parts[1][:, :HALF]], 1),
                            cat([parts[0][:, HALF:], parts[1][:, HALF:]], 1),
                        )
                    )
                (tr, ti), (br, bi) = res
                cosine = cat([sub_tw[0, pl.ds(i, ROWS), :]] * 2, 1)
                sine = cat([sub_tw[1, pl.ds(i, ROWS), :]] * 2, 1)
                dr, di = tr - br, ti - bi
                for part, real, imag in (
                    (0, tr + br, ti + bi),
                    (1, dr * cosine + di * sine, di * cosine - dr * sine),
                ):
                    for start, value in ((0, real), (HALF, imag)):
                        high, low = split(value)
                        at = (2 * k + part, pl.ds(start + i, ROWS), slice(None))
                        yh[at] = high
                        yl[at] = low

        for part in range(2):
            far = [
                dot(
                    cat([lh[...], lh[...], ll[...]], 1),
                    cat([yh[2 * k + part], yl[2 * k + part], yh[2 * k + part]], 0),
                )
                for k in range(2)
            ]
            for i in range(0, HALF, ROWS):
                pieces = [(f[i : i + ROWS], f[HALF + i : HALF + i + ROWS]) for f in far]
                total = sum(a * a + b * b for a, b in pieces)
                total = jnp.maximum(total * (1.0 / 65536.0), 0.25)
                factor = amp[pl.ds(part * HALF + i, ROWS), :] * lax.rsqrt(total) - 1.0
                factor = factor * (1.0 / 65536.0)
                for k in range(2):
                    for start, value in ((0, pieces[k][0]), (HALF, pieces[k][1])):
                        high, low = split(value * factor)
                        at = (2 * k + part, pl.ds(start + i, ROWS), slice(None))
                        yh[at] = high
                        yl[at] = low
        for k in range(2):
            near = [
                dot(
                    cat([rh[...], rh[...], rl[...]], 1),
                    cat([yh[2 * k + part], yl[2 * k + part], yh[2 * k + part]], 0),
                )
                for part in range(2)
            ]
            for i in range(0, HALF, ROWS):
                (ar, ai), (br, bi) = ((f[i : i + ROWS], f[HALF + i : HALF + i + ROWS]) for f in near)
                cosine = cat([sub_tw[0, pl.ds(i, ROWS), :]] * 2, 1)
                sine = cat([sub_tw[1, pl.ds(i, ROWS), :]] * 2, 1)
                br, bi = br * cosine - bi * sine, bi * cosine + br * sine
                for row, real, imag in ((i, ar + br, ai + bi), (HALF + i, ar - br, ai - bi)):
                    for part in range(2):
                        cols = slice(part * HALF, (part + 1) * HALF)
                        high, low = split(cat([real[:, cols], imag[:, cols]], 1))
                        at = pl.ds((2 * k + part) * EDGE + row, ROWS)
                        xh[at, :] = high
                        xl[at, :] = low

        left_hhl = cat([lh[...], lh[...], ll[...]], 0)
        whole[...] = dot(cat([xh[...], xl[...], xh[...]], 1), left_hhl)
        for i in range(0, EDGE, ROWS):
            s = pl.ds(i, ROWS)
            update = [[0.0, 0.0], [0.0, 0.0]]
            cosine, sine = lane_tw[0, :1, :], lane_tw[1, :1, :]
            for k in range(2):
                parts = [whole[pl.ds((2 * k + part) * EDGE + i, ROWS), :] for part in range(2)]
                ar, ai = parts[0][:, :HALF], parts[0][:, HALF:]
                br, bi = parts[1][:, :HALF], parts[1][:, HALF:]
                br, bi = br * cosine - bi * sine, bi * cosine + br * sine
                for h, real, imag in ((0, ar + br, ai + bi), (1, ar - br, ai - bi)):
                    cols = pl.ds(h * HALF, HALF)
                    pr, pi = probe[0, k, s, cols], probe[1, k, s, cols]
                    update[0][h] += pr * real + pi * imag
                    update[1][h] += pr * imag - pi * real
                    vr, vi = patch[0, s, cols], patch[1, s, cols]
                    sums[k, s, cols] += vr * real + vi * imag
                    sums[2 + k, s, cols] += vr * imag - vi * real
                    if k == 0:
                        sums[4, s, cols] += vr * vr + vi * vi
            for plane in range(2):
                for b, block in enumerate(spread(*update[plane], down, shift)):
                    at = (plane, pl.ds(first + i, ROWS + 8), pl.ds(base + b * HALF, HALF))
                    grad[at] += block
        return 0

    lax.fori_loop(0, metas[4, 0, 2 * SLOTS], visit, 0)


def tile_terms(place, metas, framed, probe, amps):
    vmem = pl.BlockSpec(memory_space=pltpu.VMEM)
    smem = pl.BlockSpec(memory_space=pltpu.SMEM)
    f32, bf16 = jnp.float32, jnp.bfloat16
    consts = tables()
    return pl.pallas_call(
        tile_kernel,
        out_shape=(
            jax.ShapeDtypeStruct((2, EXT, EXT), f32),
            jax.ShapeDtypeStruct((TILE, TILE), f32),
            jax.ShapeDtypeStruct((5, EDGE, EDGE), f32),
        ),
        in_specs=[smem, smem] + [vmem] * (3 + len(consts)),
        out_specs=(vmem, vmem, vmem),
        scratch_shapes=[
            pltpu.VMEM((2, EDGE, EDGE), f32),
            pltpu.VMEM((4 * EDGE, EDGE), bf16),
            pltpu.VMEM((4 * EDGE, EDGE), bf16),
            pltpu.VMEM((4, EDGE, EDGE), bf16),
            pltpu.VMEM((4, EDGE, EDGE), bf16),
            pltpu.VMEM((EDGE, EDGE), f32),
            pltpu.VMEM((LIT, LIT_PAD), f32),
            pltpu.VMEM((EDGE, EDGE), f32),
            pltpu.VMEM((4 * EDGE, EDGE), f32),
        ],
        compiler_params=pltpu.CompilerParams(vmem_limit_bytes=40 * 1024 * 1024),
        name="tile",
    )(place, metas, framed, probe, amps, *consts)


RIM_SOURCE = {-1: (0, MARGIN), 0: (MARGIN, TILE), 1: (MARGIN + TILE, MARGIN)}
RIM_TARGET = {1: (0, MARGIN), 0: (0, TILE), -1: (TILE - MARGIN, MARGIN)}


def torus_place():
    row, col = lax.axis_index("row"), lax.axis_index("col")
    return (
        row // 8,
        lax.rem(row, 4),
        (col // 2) * 2 + lax.rem(row // 4, 2),
        lax.rem(col, 2),
    )


def torus_device(x, y, z, core):
    return (x * 8 + lax.rem(z, 2) * 4 + y, (z // 2) * 2 + core)


def fold_kernel(
    grad, field, shade, sums, probe, object_out, probe_out,
    base, rims_r, rims_c, rims_d, pair_in, x_in, y_in, z_in, acc, rows_out, row_new, rows_in, spread,
    local_sems, rim_send, rim_recv, red_send, red_recv, put_send, put_recv,
):
    f32 = jnp.float32
    x, y, z, core = torus_place()
    pair = torus_device(x, y, z, 1 - core)
    x_peers = [torus_device(lax.rem(x + d, 4), y, z, core) for d in range(1, 4)]
    y_peers = [torus_device(x, lax.rem(y + d, 4), z, core) for d in range(1, 4)]
    z_peers = [torus_device(x, y, lax.rem(z + d, 8), core) for d in range(1, 8)]

    def ref_of(n):
        if n < 2:
            return rims_c.at[n]
        if n < 6:
            return rims_d.at[n - 2]
        return rims_r.at[n - 6]

    barrier = pltpu.get_barrier_semaphore()
    partners = [shifted(dr, dc) for dr, dc in NEIGHBOURS] + [pair] + x_peers + y_peers + z_peers
    for device in partners:
        pl.semaphore_signal(barrier, inc=1, device_id=device, device_id_type=MESH)
    locals_ = [
        pltpu.make_async_copy(field, base, local_sems.at[0]),
    ]
    pl.semaphore_wait(barrier, len(partners))

    def send(src, dst, device, sems, n):
        copy = pltpu.make_async_remote_copy(
            src_ref=src,
            dst_ref=dst,
            send_sem=sems[0].at[n],
            recv_sem=sems[1].at[n],
            device_id=device,
            device_id_type=MESH,
        )
        copy.start()
        return copy

    red, put = (red_send, red_recv), (put_send, put_recv)
    half = pl.multiple_of(core * HALF, HALF)
    other = pl.multiple_of((1 - core) * HALF, HALF)
    to_pair = send(sums.at[:, pl.ds(other, HALF), :], pair_in, pair, red, 0)
    rims = []
    for n, (dr, dc) in enumerate(NEIGHBOURS):
        src = grad.at[:, pl.ds(*RIM_SOURCE[dr]), pl.ds(*RIM_SOURCE[dc])]
        rims.append(send(src, ref_of(n), shifted(dr, dc), (rim_send, rim_recv), n))
    for copy in locals_:
        copy.start()

    to_pair.wait()
    for i in range(0, HALF, ROWS):
        rows = pl.ds(i, ROWS)
        acc[:, rows, :] = sums[:, pl.ds(pl.multiple_of(half + i, ROWS), ROWS), :] + pair_in[:, rows, :]
    copies = []
    for d in range(1, 4):
        at = pl.multiple_of(lax.rem(x + d, 4) * 32, 32)
        copies.append(send(acc.at[:, pl.ds(at, 32), :], x_in.at[d - 1], x_peers[d - 1], red, d))
    for copy in copies:
        copy.wait()
    x_at = pl.multiple_of(x * 32, 32)
    mine = acc[:, pl.ds(x_at, 32), :]
    for d in range(3):
        mine = mine + x_in[d]
    acc[:, pl.ds(x_at, 32), :] = mine
    copies = []
    for d in range(1, 4):
        at = pl.multiple_of(x_at + lax.rem(y + d, 4) * 8, 8)
        copies.append(send(acc.at[:, pl.ds(at, 8), :], y_in.at[d - 1], y_peers[d - 1], red, 3 + d))
    for copy in copies:
        copy.wait()
    y_at = pl.multiple_of(x_at + y * 8, 8)
    mine = acc[:, pl.ds(y_at, 8), :]
    for d in range(3):
        mine = mine + y_in[d]
    rows_out[...] = jnp.zeros_like(rows_out)
    for r in range(8):
        for p in range(5):
            rows_out[r, pl.ds(p, 1), :] = mine[p, r : r + 1, :]
    copies = []
    for d in range(1, 8):
        copies.append(send(rows_out.at[lax.rem(z + d, 8)], z_in.at[d - 1], z_peers[d - 1], red, 6 + d))
    for copy in copies:
        copy.wait()
    total = rows_out[z]
    for d in range(7):
        total = total + z_in[d]
    row_new[...] = total / (total[4:5] + 1.0)

    copies = []
    for d in range(1, 8):
        copies.append(send(row_new, rows_in.at[z], z_peers[d - 1], put, d))
    rows_in[z] = row_new[...]
    for copy in copies:
        copy.wait()
    at = pl.multiple_of(half + y_at, 8)
    for p in range(4):
        spread[p, pl.ds(at, 8), :] = jnp.concatenate([rows_in[r, pl.ds(p, 1), :] for r in range(8)], 0)
    copies = []
    block = spread.at[:, pl.ds(at, 8), :]
    for d in range(1, 4):
        copies.append(send(block, block, y_peers[d - 1], put, 7 + d))
    for copy in copies:
        copy.wait()
    block = spread.at[:, pl.ds(pl.multiple_of(half + x_at, 32), 32), :]
    copies = []
    for d in range(1, 4):
        copies.append(send(block, block, x_peers[d - 1], put, 10 + d))
    for copy in copies:
        copy.wait()
    block = spread.at[:, pl.ds(half, HALF), :]
    last = send(block, block, pair, put, 0)

    for copy in locals_:
        copy.wait()
    for n, (dr, dc) in enumerate(NEIGHBOURS):
        rims[n].wait()
        (r0, rn), (c0, cn) = RIM_TARGET[dr], RIM_TARGET[dc]
        for i in range(0, rn, 64):
            rows = pl.ds(r0 + i, 64)
            base[:, rows, pl.ds(c0, cn)] += ref_of(n)[:, pl.ds(i, 64), :] * shade[rows, pl.ds(c0, cn)]
    for i in range(0, TILE, ROWS):
        rows = pl.ds(i, ROWS)
        for c in range(2):
            object_out[c, rows, :] = (
                base[c, rows, :]
                + grad[c, pl.ds(MARGIN + i, ROWS), pl.ds(MARGIN, TILE)] * shade[rows, :]
            )
    last.wait()
    for c in range(2):
        for k in range(2):
            probe_out[c, k] = probe[c, k] + spread[2 * c + k]


def fold(grad, field, shade, sums, probe):
    vmem = pl.BlockSpec(memory_space=pltpu.VMEM)
    any_spec = pl.BlockSpec(memory_space=pl.ANY)
    f32 = jnp.float32
    dma = pltpu.SemaphoreType.DMA
    return pl.pallas_call(
        fold_kernel,
        out_shape=(
            jax.ShapeDtypeStruct((2, TILE, TILE), f32),
            jax.ShapeDtypeStruct((2, 2, EDGE, EDGE), f32),
        ),
        in_specs=[vmem, any_spec, vmem, vmem, vmem],
        out_specs=(vmem, vmem),
        scratch_shapes=[
            pltpu.VMEM((2, TILE, TILE), f32),
            pltpu.VMEM((2, 2, MARGIN, TILE), f32),
            pltpu.VMEM((2, 2, TILE, MARGIN), f32),
            pltpu.VMEM((4, 2, MARGIN, MARGIN), f32),
            pltpu.VMEM((5, HALF, EDGE), f32),
            pltpu.VMEM((3, 5, 32, EDGE), f32),
            pltpu.VMEM((3, 5, 8, EDGE), f32),
            pltpu.VMEM((7, 8, EDGE), f32),
            pltpu.VMEM((5, HALF, EDGE), f32),
            pltpu.VMEM((8, 8, EDGE), f32),
            pltpu.VMEM((8, EDGE), f32),
            pltpu.VMEM((8, 8, EDGE), f32),
            pltpu.VMEM((4, EDGE, EDGE), f32),
            dma((1,)), dma((8,)), dma((8,)), dma((14,)), dma((14,)), dma((14,)), dma((14,)),
        ],
        compiler_params=pltpu.CompilerParams(
            collective_id=1, has_side_effects=True, vmem_limit_bytes=32 * 1024 * 1024
        ),
        name="fold",
    )(grad, field, shade, sums, probe)


def on_device(field, probe, offsets, counts, amps):
    row, col = lax.axis_index("row"), lax.axis_index("col")
    meta = jnp.concatenate([offsets.reshape(2 * SLOTS), counts.reshape(1)])
    meta = jnp.broadcast_to(jnp.pad(meta, (0, 128 - 2 * SLOTS - 1))[None], (8, 128))
    framed, metas = gather_frame(field, meta)
    place = jnp.stack([row * TILE, col * TILE]).astype(jnp.int32)
    grad, shade, sums = tile_terms(place, metas, framed, probe, amps[0, 0])
    return fold(grad, field, shade, sums, probe)


def solution(mesh):
    in_specs = (
        P(None, "row", "col"),
        P(),
        P("row", "col", None, None),
        P("row", "col"),
        P("row", "col", None, None, None),
    )
    out_specs = (P(None, "row", "col"), P())
    return jax.shard_map(
        on_device, mesh=mesh, in_specs=in_specs, out_specs=out_specs, check_vma=False
    )
```

```python
import functools
import math

import jax
import jax.numpy as jnp
import numpy as np
from jax import lax
from jax.experimental import pallas as pl
from jax.experimental.pallas import tpu as pltpu
from jax.sharding import PartitionSpec as P

MESH = pl.DeviceIdType.MESH
EDGE = 256
HALF = 128
TILE = 512
MARGIN = 128
EXT = TILE + 2 * MARGIN
SLOTS = 6
SIDES = tuple((dr, dc) for dr in (-1, 0, 1) for dc in (-1, 0, 1))
NEIGHBOURS = ((0, 1), (0, -1), (1, 1), (1, -1), (-1, 1), (-1, -1), (1, 0), (-1, 0))
LIT = 1024
LIT_PAD = LIT + 128
ROWS = 32


def shifted(dr, dc):
    rows, cols = lax.axis_size("row"), lax.axis_size("col")
    row = lax.rem(lax.axis_index("row") + dr + rows, rows)
    col = lax.rem(lax.axis_index("col") + dc + cols, cols)
    return (row, col)


def edge_span(step):
    if step == 0:
        return pl.ds(0, TILE), pl.ds(MARGIN, TILE)
    if step > 0:
        return pl.ds(TILE - MARGIN, MARGIN), pl.ds(0, MARGIN)
    return pl.ds(0, MARGIN), pl.ds(MARGIN + TILE, MARGIN)


def relays(down):
    y = lax.rem(lax.axis_index("row"), 4)
    return (y == 3, y == 2) if down == 1 else (y == 0, y == 1)


def start_either(direct, detour, taken):
    pl.when(taken)(detour.start)
    pl.when(jnp.logical_not(taken))(direct.start)


BESIDE = ((0, 1), (0, -1))
PARTNERS = BESIDE + ((1, 0), (-1, 0), (2, 0), (-2, 0))
ENDS = (0, TILE - MARGIN)
MIDDLE = pl.ds(MARGIN, TILE - 2 * MARGIN)
PIECE = MARGIN // 2


def halo_kernel(
    field, meta, framed, metas, relay, local_sems, side_send, side_recv, end_send, end_recv,
    mid_send, mid_recv, relay_recv, on_send, corner_send, corner_recv, meta_send, meta_recv,
):
    greeted = PARTNERS + ((1, 1), (1, -1), (-1, 1), (-1, -1))
    barrier = pltpu.get_barrier_semaphore()
    for dr, dc in greeted:
        pl.semaphore_signal(barrier, inc=1, device_id=shifted(dr, dc), device_id_type=MESH)
    own = pltpu.make_async_copy(
        field, framed.at[:, pl.ds(MARGIN, TILE), pl.ds(MARGIN, TILE)], local_sems.at[0]
    )
    own_meta = pltpu.make_async_copy(meta, metas.at[4], local_sems.at[1])
    pl.semaphore_wait(barrier, len(greeted))

    def remote(src, dst, send_sem, recv_sem, device):
        return pltpu.make_async_remote_copy(
            src_ref=src, dst_ref=dst, send_sem=send_sem, recv_sem=recv_sem,
            device_id=device, device_id_type=MESH,
        )

    copies = []
    for n, (dr, dc) in enumerate(NEIGHBOURS):
        copies.append(
            remote(
                meta, metas.at[SIDES.index((-dr, -dc))], meta_send.at[n], meta_recv.at[n],
                shifted(dr, dc),
            )
        )
    ends, middles = {}, {}
    for d, dr in enumerate((1, -1)):
        src_r, dst_r = edge_span(dr)
        for e, lane in enumerate(ENDS):
            ends[dr, e] = remote(
                field.at[:, src_r, pl.ds(lane, MARGIN)],
                framed.at[:, dst_r, pl.ds(MARGIN + lane, MARGIN)],
                end_send.at[d, e], end_recv.at[d, e], shifted(dr, 0),
            )
            ends[dr, e].start()
    for d, dr in enumerate((1, -1)):
        src_r, dst_r = edge_span(dr)
        taken, _ = relays(dr)
        for i in range(2):
            src = field.at[:, pl.ds(src_r.start + i * PIECE, PIECE), MIDDLE]
            middles[dr, i] = remote(
                src,
                framed.at[:, pl.ds(dst_r.start + i * PIECE, PIECE), pl.ds(2 * MARGIN, MIDDLE.size)],
                mid_send.at[d, i], mid_recv.at[d, i], shifted(dr, 0),
            )
            detour = remote(
                src, relay.at[i], mid_send.at[d, i], relay_recv.at[i], shifted(-dr, 0)
            )
            start_either(middles[dr, i], detour, taken)
    for d, (dr, dc) in enumerate(BESIDE):
        src_c, dst_c = edge_span(dc)
        side = remote(
            field.at[:, :, src_c], framed.at[:, pl.ds(MARGIN, TILE), dst_c],
            side_send.at[d], side_recv.at[d], shifted(dr, dc),
        )
        copies.append(side)
    for copy in copies:
        copy.start()
    own.start()
    own_meta.start()
    for d, dr in enumerate((1, -1)):
        _, rows = edge_span(dr)
        for e, dc in enumerate((-1, 1)):
            ends[dr, e].wait()
            _, lanes = edge_span(dc)
            corner = remote(
                framed.at[:, rows, pl.ds(MARGIN + ENDS[e], MARGIN)], framed.at[:, rows, lanes],
                corner_send.at[d, e], corner_recv.at[d, e], shifted(0, dc),
            )
            corner.start()
            copies.append(corner)
    onward = {}
    for d, dr in enumerate((1, -1)):
        _, handed = relays(dr)
        _, dst_r = edge_span(dr)
        for i in range(2):
            onward[dr, i] = remote(
                relay.at[i],
                framed.at[:, pl.ds(dst_r.start + i * PIECE, PIECE), pl.ds(2 * MARGIN, MIDDLE.size)],
                on_send.at[i], mid_recv.at[d, i], shifted(2 * dr, 0),
            )
            arrived = remote(
                relay.at[i], relay.at[i], on_send.at[i], relay_recv.at[i], shifted(2 * dr, 0)
            )

            @pl.when(handed)
            def _():
                arrived.wait_recv()
                onward[dr, i].start()

    own.wait()
    own_meta.wait()
    for copy in copies:
        copy.wait()
    for copy in middles.values():
        copy.wait()
    for (dr, _), copy in onward.items():
        pl.when(relays(dr)[1])(copy.wait_send)


def gather_frame(field, meta):
    any_spec = pl.BlockSpec(memory_space=pl.ANY)
    count = len(NEIGHBOURS)
    vmem = pl.BlockSpec(memory_space=pltpu.VMEM)
    dma = pltpu.SemaphoreType.DMA
    return pl.pallas_call(
        halo_kernel,
        out_shape=(
            jax.ShapeDtypeStruct((2, EXT, EXT), jnp.float32),
            jax.ShapeDtypeStruct((9, 8, 128), jnp.int32),
        ),
        in_specs=[pl.BlockSpec(memory_space=pltpu.HBM), any_spec],
        out_specs=(vmem, any_spec),
        scratch_shapes=[
            pltpu.VMEM((2, 2, PIECE, MIDDLE.size), jnp.float32),
            dma((2,)), dma((2,)), dma((2,)), dma((2, 2)), dma((2, 2)), dma((2, 2)), dma((2, 2)),
            dma((2,)), dma((2,)), dma((2, 2)), dma((2, 2)), dma((count,)), dma((count,)),
        ],
        compiler_params=pltpu.CompilerParams(
            collective_id=0, has_side_effects=True, vmem_limit_bytes=16 * 1024 * 1024
        ),
        name="halo",
    )(field, meta)


def split(x):
    high = x.astype(jnp.bfloat16)
    return high, (x - high.astype(jnp.float32)).astype(jnp.bfloat16)


def tables():
    n = np.arange(HALF)
    angle = 2.0 * np.pi * ((n[:, None] * n[None, :]) % HALF) / HALF
    cosine, sine = np.cos(angle), np.sin(angle)
    right = np.block([[cosine, -sine], [sine, cosine]]).astype(np.float32)
    half_angle = 2.0 * np.pi * n / EDGE
    twist = np.stack([np.cos(half_angle), np.sin(half_angle)]).astype(np.float32)
    lanes = np.broadcast_to(twist[:, None, :], (2, 8, HALF))
    subs = np.broadcast_to(twist[:, :, None], (2, HALF, HALF))
    order = np.concatenate([np.arange(0, EDGE, 2), np.arange(1, EDGE, 2)])
    pick = (order[:, None] == np.arange(EDGE)[None, :]).astype(np.float32)
    out = []
    for table in (right, right.T):
        high = table.astype(jnp.bfloat16)
        out += [high, (table - high.astype(np.float32)).astype(jnp.bfloat16)]
    out += [pick.astype(jnp.bfloat16), pick.T.astype(jnp.bfloat16)]
    twists = np.concatenate([subs, lanes], 1)
    return [jnp.asarray(np.stack(out)), jnp.asarray(twists)]


def cat(parts, axis):
    return jnp.concatenate(parts, axis=axis)


def tile_kernel(
    place, metas, framed, probe, amps, mats, twists,
    grad, shade, sums,
    patch, xh, xl, yh, yl, amp, light, power, whole,
):
    f32, bf16 = jnp.float32, jnp.bfloat16
    dot = functools.partial(jnp.dot, preferred_element_type=f32)
    lane = lax.broadcasted_iota(jnp.int32, (1, HALF), 1)
    top, left = place[0], place[1]
    rh, rl, lh, ll, pick, pick_t = (mats.at[n] for n in range(6))
    sub_tw, lane_tw = twists.at[:, pl.ds(0, HALF), :], twists.at[:, pl.ds(HALF, 8), :]

    grad[...] = jnp.zeros_like(grad)
    sums[...] = jnp.zeros_like(sums)
    for i in range(0, EDGE, ROWS):
        s = pl.ds(i, ROWS)
        power[s, :] = sum(probe[c, k, s, :] * probe[c, k, s, :] for k in range(2) for c in range(2))
    light[pl.ds(256, TILE), pl.ds(256, TILE)] = jnp.zeros((TILE, TILE), f32)

    def spread(low, high, down, shift):
        below = jnp.zeros((8, HALF), f32)
        low, high = (
            pltpu.roll(pltpu.roll(cat([v, below], 0), down, 0), shift, 1) for v in (low, high)
        )
        keep = lane >= shift
        return (
            jnp.where(keep, low, 0.0),
            jnp.where(keep, high, low),
            jnp.where(keep, 0.0, high),
        )

    def light_slot(which, position):
        r = metas[which, 0, position] - top + 256
        c = metas[which, 1, position] - left + 256

        @pl.when((r > 0) & (r < 768) & (c > 0) & (c < 768))
        def _():
            shift, down = lax.rem(c, HALF), lax.rem(r, 8)
            base = pl.multiple_of(c - shift, HALF)
            first = pl.multiple_of(r - down, 8)
            for i in range(0, EDGE, ROWS):
                s = pl.ds(i, ROWS)
                blocks = spread(power[s, :HALF], power[s, HALF:], down, shift)
                for b, block in enumerate(blocks):
                    at = (pl.ds(first + i, ROWS + 8), pl.ds(base + b * HALF, HALF))
                    light[at] += block

    def light_tile(which, _):
        def one(position, _):
            light_slot(which, position)
            return 0

        lax.fori_loop(0, metas[which, 2, 0], one, 0)
        return 0

    lax.fori_loop(0, 9, light_tile, 0)
    for i in range(0, TILE, ROWS):
        shade[pl.ds(i, ROWS), :] = 1.0 / (light[pl.ds(256 + i, ROWS), pl.ds(256, TILE)] + 1.0)

    right_hhl = cat([rh[...], rh[...], rl[...]], 0)

    def visit(position, _):
        r = metas[4, 0, position] - top + MARGIN
        c = metas[4, 1, position] - left + MARGIN
        shift = lax.rem(c, HALF)
        base = pl.multiple_of(c - shift, HALF)
        down = lax.rem(r, 8)
        first = pl.multiple_of(r - down, 8)
        up = lax.rem(ROWS + 8 - down, ROWS + 8)
        back_shift = lax.rem(HALF - shift, HALF)
        keep = lane < HALF - shift
        picked = dot(pick[...], amps[position]).astype(bf16)
        amp[...] = dot(picked, pick_t[...])

        for i in range(0, EDGE, ROWS):
            s = pl.ds(i, ROWS)
            planes = []
            for plane in range(2):
                rolled = [
                    pltpu.roll(
                        pltpu.roll(
                            framed[
                                plane, pl.ds(first + i, ROWS + 8), pl.ds(base + b * HALF, HALF)
                            ],
                            up,
                            0,
                        )[:ROWS],
                        back_shift,
                        1,
                    )
                    for b in range(3)
                ]
                planes.append(
                    (jnp.where(keep, rolled[0], rolled[1]), jnp.where(keep, rolled[1], rolled[2]))
                )
            for plane in range(2):
                for h in range(2):
                    patch[plane, s, pl.ds(h * HALF, HALF)] = planes[plane][h]
            for k in range(2):
                wr, wi = [], []
                for h in range(2):
                    pr, pi = (probe[p, k, s, pl.ds(h * HALF, HALF)] for p in range(2))
                    wr.append(pr * planes[0][h] - pi * planes[1][h])
                    wi.append(pr * planes[1][h] + pi * planes[0][h])
                cosine, sine = lane_tw[0, :1, :], lane_tw[1, :1, :]
                dr, di = wr[0] - wr[1], wi[0] - wi[1]
                for part, value in (
                    (0, cat([wr[0] + wr[1], wi[0] + wi[1]], 1)),
                    (1, cat([dr * cosine + di * sine, di * cosine - dr * sine], 1)),
                ):
                    high, low = split(value)
                    at = pl.ds((2 * k + part) * EDGE + i, ROWS)
                    xh[at, :] = high
                    xl[at, :] = low

        whole[...] = dot(cat([xh[...], xl[...], xh[...]], 1), right_hhl)
        for k in range(2):
            for i in range(0, HALF, ROWS):
                res = []
                for row in (i, HALF + i):
                    parts = [
                        whole[pl.ds((2 * k + part) * EDGE + row, ROWS), :] for part in range(2)
                    ]
                    res.append(
                        (
                            cat([parts[0][:, :HALF], parts[1][:, :HALF]], 1),
                            cat([parts[0][:, HALF:], parts[1][:, HALF:]], 1),
                        )
                    )
                (tr, ti), (br, bi) = res
                cosine = cat([sub_tw[0, pl.ds(i, ROWS), :]] * 2, 1)
                sine = cat([sub_tw[1, pl.ds(i, ROWS), :]] * 2, 1)
                dr, di = tr - br, ti - bi
                for part, real, imag in (
                    (0, tr + br, ti + bi),
                    (1, dr * cosine + di * sine, di * cosine - dr * sine),
                ):
                    for start, value in ((0, real), (HALF, imag)):
                        high, low = split(value)
                        at = (2 * k + part, pl.ds(start + i, ROWS), slice(None))
                        yh[at] = high
                        yl[at] = low

        for part in range(2):
            far = [
                dot(
                    cat([lh[...], lh[...], ll[...]], 1),
                    cat([yh[2 * k + part], yl[2 * k + part], yh[2 * k + part]], 0),
                )
                for k in range(2)
            ]
            for i in range(0, HALF, ROWS):
                pieces = [(f[i : i + ROWS], f[HALF + i : HALF + i + ROWS]) for f in far]
                total = sum(a * a + b * b for a, b in pieces)
                total = jnp.maximum(total * (1.0 / 65536.0), 0.25)
                factor = amp[pl.ds(part * HALF + i, ROWS), :] * lax.rsqrt(total) - 1.0
                factor = factor * (1.0 / 65536.0)
                for k in range(2):
                    for start, value in ((0, pieces[k][0]), (HALF, pieces[k][1])):
                        high, low = split(value * factor)
                        at = (2 * k + part, pl.ds(start + i, ROWS), slice(None))
                        yh[at] = high
                        yl[at] = low
        for k in range(2):
            near = [
                dot(
                    cat([rh[...], rh[...], rl[...]], 1),
                    cat([yh[2 * k + part], yl[2 * k + part], yh[2 * k + part]], 0),
                )
                for part in range(2)
            ]
            for i in range(0, HALF, ROWS):
                (ar, ai), (br, bi) = ((f[i : i + ROWS], f[HALF + i : HALF + i + ROWS]) for f in near)
                cosine = cat([sub_tw[0, pl.ds(i, ROWS), :]] * 2, 1)
                sine = cat([sub_tw[1, pl.ds(i, ROWS), :]] * 2, 1)
                br, bi = br * cosine - bi * sine, bi * cosine + br * sine
                for row, real, imag in ((i, ar + br, ai + bi), (HALF + i, ar - br, ai - bi)):
                    for part in range(2):
                        cols = slice(part * HALF, (part + 1) * HALF)
                        high, low = split(cat([real[:, cols], imag[:, cols]], 1))
                        at = pl.ds((2 * k + part) * EDGE + row, ROWS)
                        xh[at, :] = high
                        xl[at, :] = low

        left_hhl = cat([lh[...], lh[...], ll[...]], 0)
        whole[...] = dot(cat([xh[...], xl[...], xh[...]], 1), left_hhl)
        for i in range(0, EDGE, ROWS):
            s = pl.ds(i, ROWS)
            update = [[0.0, 0.0], [0.0, 0.0]]
            cosine, sine = lane_tw[0, :1, :], lane_tw[1, :1, :]
            for k in range(2):
                parts = [whole[pl.ds((2 * k + part) * EDGE + i, ROWS), :] for part in range(2)]
                ar, ai = parts[0][:, :HALF], parts[0][:, HALF:]
                br, bi = parts[1][:, :HALF], parts[1][:, HALF:]
                br, bi = br * cosine - bi * sine, bi * cosine + br * sine
                for h, real, imag in ((0, ar + br, ai + bi), (1, ar - br, ai - bi)):
                    cols = pl.ds(h * HALF, HALF)
                    pr, pi = probe[0, k, s, cols], probe[1, k, s, cols]
                    update[0][h] += pr * real + pi * imag
                    update[1][h] += pr * imag - pi * real
                    vr, vi = patch[0, s, cols], patch[1, s, cols]
                    sums[k, s, cols] += vr * real + vi * imag
                    sums[2 + k, s, cols] += vr * imag - vi * real
                    if k == 0:
                        sums[4, s, cols] += vr * vr + vi * vi
            for plane in range(2):
                for b, block in enumerate(spread(*update[plane], down, shift)):
                    at = (plane, pl.ds(first + i, ROWS + 8), pl.ds(base + b * HALF, HALF))
                    grad[at] += block
        return 0

    lax.fori_loop(0, metas[4, 2, 0], visit, 0)


def tile_terms(place, metas, framed, probe, amps):
    vmem = pl.BlockSpec(memory_space=pltpu.VMEM)
    smem = pl.BlockSpec(memory_space=pltpu.SMEM)
    f32, bf16 = jnp.float32, jnp.bfloat16
    consts = tables()
    return pl.pallas_call(
        tile_kernel,
        out_shape=(
            jax.ShapeDtypeStruct((2, EXT, EXT), f32),
            jax.ShapeDtypeStruct((TILE, TILE), f32),
            jax.ShapeDtypeStruct((5, EDGE, EDGE), f32),
        ),
        in_specs=[smem, smem] + [vmem] * (3 + len(consts)),
        out_specs=(vmem, vmem, vmem),
        scratch_shapes=[
            pltpu.VMEM((2, EDGE, EDGE), f32),
            pltpu.VMEM((4 * EDGE, EDGE), bf16),
            pltpu.VMEM((4 * EDGE, EDGE), bf16),
            pltpu.VMEM((4, EDGE, EDGE), bf16),
            pltpu.VMEM((4, EDGE, EDGE), bf16),
            pltpu.VMEM((EDGE, EDGE), f32),
            pltpu.VMEM((LIT, LIT_PAD), f32),
            pltpu.VMEM((EDGE, EDGE), f32),
            pltpu.VMEM((4 * EDGE, EDGE), f32),
        ],
        compiler_params=pltpu.CompilerParams(vmem_limit_bytes=40 * 1024 * 1024),
        name="tile",
    )(place, metas, framed, probe, amps, *consts)


RIM_SOURCE = {-1: (0, MARGIN), 0: (MARGIN, TILE), 1: (MARGIN + TILE, MARGIN)}
CORNERS = (2, 3, 4, 5)
PIECES = tuple(
    piece for i in range(4) for piece in ((0, i), (1, i), (CORNERS[i], 0), (6, i), (7, i))
)
SLOT = (5, 4, 3, 2, 2, 2, 2)
RIM_TARGET = {1: (0, MARGIN), 0: (0, TILE), -1: (TILE - MARGIN, MARGIN)}


def torus_place():
    row, col = lax.axis_index("row"), lax.axis_index("col")
    return (
        row // 8,
        lax.rem(row, 4),
        (col // 2) * 2 + lax.rem(row // 4, 2),
        lax.rem(col, 2),
    )


def torus_device(x, y, z, core):
    return (x * 8 + lax.rem(z, 2) * 4 + y, (z // 2) * 2 + core)


def fold_kernel(
    grad, field, shade, sums, probe, object_out, probe_out,
    base, rims_r, rims_c, rims_d, pair_in, x_in, y_in, z_in, acc, rows_out, row_new, rows_in, spread,
    local_sems, rim_send, rim_recv, red_send, red_recv, put_send, put_recv,
):
    f32 = jnp.float32
    x, y, z, core = torus_place()
    pair = torus_device(x, y, z, 1 - core)
    x_peers = [torus_device(lax.rem(x + d, 4), y, z, core) for d in range(1, 4)]
    y_peers = [torus_device(x, lax.rem(y + d, 4), z, core) for d in range(1, 4)]
    z_peers = [torus_device(x, y, lax.rem(z + d, 8), core) for d in range(1, 8)]

    def ref_of(n):
        if n < 2:
            return rims_c.at[n]
        if n < 6:
            return rims_d.at[n - 2]
        return rims_r.at[n - 6]

    barrier = pltpu.get_barrier_semaphore()
    partners = [shifted(dr, dc) for dr, dc in NEIGHBOURS] + [pair] + x_peers + y_peers + z_peers
    for device in partners:
        pl.semaphore_signal(barrier, inc=1, device_id=device, device_id_type=MESH)
    locals_ = [
        pltpu.make_async_copy(field, base, local_sems.at[0]),
    ]
    pl.semaphore_wait(barrier, len(partners))

    def send(src, dst, device, sems, n):
        copy = pltpu.make_async_remote_copy(
            src_ref=src,
            dst_ref=dst,
            send_sem=sems[0].at[n],
            recv_sem=sems[1].at[n],
            device_id=device,
            device_id_type=MESH,
        )
        copy.start()
        return copy

    red, put = (red_send, red_recv), (put_send, put_recv)
    half = pl.multiple_of(core * HALF, HALF)
    other = pl.multiple_of((1 - core) * HALF, HALF)
    to_pair = send(sums.at[:, pl.ds(other, HALF), :], pair_in, pair, red, 0)
    rims = []

    def send_rims(count):
        for n, i in PIECES[len(rims) : len(rims) + count]:
            dr, dc = NEIGHBOURS[n]
            (r0, rn), (c0, cn) = RIM_SOURCE[dr], RIM_SOURCE[dc]
            size = rn if n in CORNERS else rn // 4
            src = grad.at[:, pl.ds(r0 + i * size, size), pl.ds(c0, cn)]
            dst = ref_of(n).at[:, pl.ds(i * size, size), :]
            rims.append(send(src, dst, shifted(dr, dc), (rim_send, rim_recv), len(rims)))

    send_rims(SLOT[0])
    for copy in locals_:
        copy.start()

    to_pair.wait()
    for i in range(0, HALF, ROWS):
        rows = pl.ds(i, ROWS)
        acc[:, rows, :] = sums[:, pl.ds(pl.multiple_of(half + i, ROWS), ROWS), :] + pair_in[:, rows, :]
    turns = ((x, x_peers, y, y_peers), (y, y_peers, x, x_peers))
    copies = []
    for d in range(1, 4):
        for h, (one, one_peers, _, _) in enumerate(turns):
            at = pl.multiple_of(lax.rem(one + d, 4) * 32, 32)
            src = acc.at[:, pl.ds(at, 32), pl.ds(h * HALF, HALF)]
            copies.append(send(src, x_in.at[h, d - 1], one_peers[d - 1], red, 3 * h + d))
    send_rims(SLOT[1])
    for copy in copies:
        copy.wait()
    copies = []
    ats = []
    for h, (one, _, two, two_peers) in enumerate(turns):
        lanes = pl.ds(h * HALF, HALF)
        at = pl.multiple_of(one * 32, 32)
        mine = acc[:, pl.ds(at, 32), lanes]
        for d in range(3):
            mine = mine + x_in[h, d]
        acc[:, pl.ds(at, 32), lanes] = mine
        ats.append((at, pl.multiple_of(at + two * 8, 8)))
        for d in range(1, 4):
            to = pl.multiple_of(at + lax.rem(two + d, 4) * 8, 8)
            src = acc.at[:, pl.ds(to, 8), lanes]
            copies.append(send(src, y_in.at[h, d - 1], two_peers[d - 1], red, 6 + 3 * h + d))
    send_rims(SLOT[2])
    for copy in copies:
        copy.wait()
    halves = []
    for h in range(2):
        part = acc[:, pl.ds(ats[h][1], 8), pl.ds(h * HALF, HALF)]
        for d in range(3):
            part = part + y_in[h, d]
        halves.append(part)
    mine = jnp.concatenate(halves, 2)
    rows_out[...] = jnp.zeros_like(rows_out)
    for r in range(8):
        for p in range(5):
            rows_out[r, pl.ds(p, 1), :] = mine[p, r : r + 1, :]
    copies = []
    for d in range(1, 8):
        copies.append(send(rows_out.at[lax.rem(z + d, 8)], z_in.at[d - 1], z_peers[d - 1], red, 12 + d))
    send_rims(SLOT[3])
    for copy in copies:
        copy.wait()
    total = rows_out[z]
    for d in range(7):
        total = total + z_in[d]
    row_new[...] = total / (total[4:5] + 1.0)

    copies = []
    for d in range(1, 8):
        copies.append(send(row_new, rows_in.at[z], z_peers[d - 1], put, d))
    rows_in[z] = row_new[...]
    send_rims(SLOT[4])
    for copy in copies:
        copy.wait()
    copies = []
    for h in range(2):
        at, lanes = pl.multiple_of(half + ats[h][1], 8), pl.ds(h * HALF, HALF)
        for p in range(4):
            spread[p, pl.ds(at, 8), lanes] = jnp.concatenate(
                [rows_in[r, pl.ds(p, 1), lanes] for r in range(8)], 0
            )
        block = spread.at[:, pl.ds(at, 8), lanes]
        for d in range(1, 4):
            copies.append(send(block, block, turns[h][3][d - 1], put, 7 + 3 * h + d))
    send_rims(SLOT[5])
    for copy in copies:
        copy.wait()
    copies = []
    for d in range(1, 4):
        for h in range(2):
            at = pl.multiple_of(half + ats[h][0], 32)
            block = spread.at[:, pl.ds(at, 32), pl.ds(h * HALF, HALF)]
            copies.append(send(block, block, turns[h][1][d - 1], put, 13 + 3 * h + d))
    send_rims(SLOT[6])
    for copy in copies:
        copy.wait()
    block = spread.at[:, pl.ds(half, HALF), :]
    last = send(block, block, pair, put, 0)

    for copy in locals_:
        copy.wait()
    for copy in rims:
        copy.wait()
    for n, (dr, dc) in enumerate(NEIGHBOURS):
        (r0, rn), (c0, cn) = RIM_TARGET[dr], RIM_TARGET[dc]
        for i in range(0, rn, 64):
            rows = pl.ds(r0 + i, 64)
            base[:, rows, pl.ds(c0, cn)] += ref_of(n)[:, pl.ds(i, 64), :] * shade[rows, pl.ds(c0, cn)]
    for i in range(0, TILE, ROWS):
        rows = pl.ds(i, ROWS)
        for c in range(2):
            object_out[c, rows, :] = (
                base[c, rows, :]
                + grad[c, pl.ds(MARGIN + i, ROWS), pl.ds(MARGIN, TILE)] * shade[rows, :]
            )
    last.wait()
    for c in range(2):
        for k in range(2):
            probe_out[c, k] = probe[c, k] + spread[2 * c + k]


def fold(grad, field, shade, sums, probe):
    vmem = pl.BlockSpec(memory_space=pltpu.VMEM)
    any_spec = pl.BlockSpec(memory_space=pl.ANY)
    f32 = jnp.float32
    dma = pltpu.SemaphoreType.DMA
    return pl.pallas_call(
        fold_kernel,
        out_shape=(
            jax.ShapeDtypeStruct((2, TILE, TILE), f32),
            jax.ShapeDtypeStruct((2, 2, EDGE, EDGE), f32),
        ),
        in_specs=[vmem, any_spec, vmem, vmem, vmem],
        out_specs=(vmem, vmem),
        scratch_shapes=[
            pltpu.VMEM((2, TILE, TILE), f32),
            pltpu.VMEM((2, 2, MARGIN, TILE), f32),
            pltpu.VMEM((2, 2, TILE, MARGIN), f32),
            pltpu.VMEM((4, 2, MARGIN, MARGIN), f32),
            pltpu.VMEM((5, HALF, EDGE), f32),
            pltpu.VMEM((2, 3, 5, 32, HALF), f32),
            pltpu.VMEM((2, 3, 5, 8, HALF), f32),
            pltpu.VMEM((7, 8, EDGE), f32),
            pltpu.VMEM((5, HALF, EDGE), f32),
            pltpu.VMEM((8, 8, EDGE), f32),
            pltpu.VMEM((8, EDGE), f32),
            pltpu.VMEM((8, 8, EDGE), f32),
            pltpu.VMEM((4, EDGE, EDGE), f32),
            dma((1,)), dma((len(PIECES),)), dma((len(PIECES),)), dma((20,)), dma((20,)), dma((20,)), dma((20,)),
        ],
        compiler_params=pltpu.CompilerParams(
            collective_id=1, has_side_effects=True, vmem_limit_bytes=32 * 1024 * 1024
        ),
        name="fold",
    )(grad, field, shade, sums, probe)


def on_device(field, probe, offsets, counts, amps):
    row, col = lax.axis_index("row"), lax.axis_index("col")
    meta = jnp.pad(offsets[0, 0], ((0, 6), (0, 128 - SLOTS))) + jnp.pad(counts, ((2, 5), (0, 127)))
    framed, metas = gather_frame(field, meta)
    place = jnp.stack([row * TILE, col * TILE]).astype(jnp.int32)
    grad, shade, sums = tile_terms(place, metas, framed, probe, amps[0, 0])
    return fold(grad, field, shade, sums, probe)


def solution(mesh):
    in_specs = (
        P(None, "row", "col"),
        P(),
        P("row", "col", None, None),
        P("row", "col"),
        P("row", "col", None, None, None),
    )
    out_specs = (P(None, "row", "col"), P())
    return jax.shard_map(
        on_device, mesh=mesh, in_specs=in_specs, out_specs=out_specs, check_vma=False
    )
```

```python
import functools
import math

import jax
import jax.numpy as jnp
import numpy as np
from jax import lax
from jax.experimental import pallas as pl
from jax.experimental.pallas import tpu as pltpu
from jax.sharding import PartitionSpec as P

MESH = pl.DeviceIdType.MESH
EDGE = 256
HALF = 128
TILE = 512
MARGIN = 128
EXT = TILE + 2 * MARGIN
SLOTS = 6
SIDES = tuple((dr, dc) for dr in (-1, 0, 1) for dc in (-1, 0, 1))
NEIGHBOURS = ((0, 1), (0, -1), (1, 1), (1, -1), (-1, 1), (-1, -1), (1, 0), (-1, 0))
LIT = 1024
LIT_PAD = LIT + 128
ROWS = 32


def shifted(dr, dc):
    rows, cols = lax.axis_size("row"), lax.axis_size("col")
    row = lax.rem(lax.axis_index("row") + dr + rows, rows)
    col = lax.rem(lax.axis_index("col") + dc + cols, cols)
    return (row, col)


def edge_span(step):
    if step == 0:
        return pl.ds(0, TILE), pl.ds(MARGIN, TILE)
    if step > 0:
        return pl.ds(TILE - MARGIN, MARGIN), pl.ds(0, MARGIN)
    return pl.ds(0, MARGIN), pl.ds(MARGIN + TILE, MARGIN)


def relays(down):
    y = lax.rem(lax.axis_index("row"), 4)
    return (y == 3, y == 2) if down == 1 else (y == 0, y == 1)


def start_either(direct, detour, taken):
    pl.when(taken)(detour.start)
    pl.when(jnp.logical_not(taken))(direct.start)


BESIDE = ((0, 1), (0, -1))
PARTNERS = BESIDE + ((1, 0), (-1, 0), (2, 0), (-2, 0))
ENDS = (0, TILE - MARGIN)
MIDDLE = pl.ds(MARGIN, TILE - 2 * MARGIN)
PIECE = MARGIN // 2


def halo_kernel(
    field, meta, framed, metas, relay, local_sems, side_send, side_recv, end_send, end_recv,
    mid_send, mid_recv, relay_recv, on_send, corner_send, corner_recv, meta_send, meta_recv,
):
    greeted = PARTNERS + ((1, 1), (1, -1), (-1, 1), (-1, -1))
    barrier = pltpu.get_barrier_semaphore()
    for dr, dc in greeted:
        pl.semaphore_signal(barrier, inc=1, device_id=shifted(dr, dc), device_id_type=MESH)
    own = pltpu.make_async_copy(
        field, framed.at[:, pl.ds(MARGIN, TILE), pl.ds(MARGIN, TILE)], local_sems.at[0]
    )
    own_meta = pltpu.make_async_copy(meta, metas.at[4], local_sems.at[1])
    pl.semaphore_wait(barrier, len(greeted))

    def remote(src, dst, send_sem, recv_sem, device):
        return pltpu.make_async_remote_copy(
            src_ref=src, dst_ref=dst, send_sem=send_sem, recv_sem=recv_sem,
            device_id=device, device_id_type=MESH,
        )

    copies = []
    for n, (dr, dc) in enumerate(NEIGHBOURS):
        copies.append(
            remote(
                meta, metas.at[SIDES.index((-dr, -dc))], meta_send.at[n], meta_recv.at[n],
                shifted(dr, dc),
            )
        )
    ends, middles = {}, {}
    for d, dr in enumerate((1, -1)):
        src_r, dst_r = edge_span(dr)
        for e, lane in enumerate(ENDS):
            ends[dr, e] = remote(
                field.at[:, src_r, pl.ds(lane, MARGIN)],
                framed.at[:, dst_r, pl.ds(MARGIN + lane, MARGIN)],
                end_send.at[d, e], end_recv.at[d, e], shifted(dr, 0),
            )
            ends[dr, e].start()
    for d, dr in enumerate((1, -1)):
        src_r, dst_r = edge_span(dr)
        taken, _ = relays(dr)
        for i in range(2):
            src = field.at[:, pl.ds(src_r.start + i * PIECE, PIECE), MIDDLE]
            middles[dr, i] = remote(
                src,
                framed.at[:, pl.ds(dst_r.start + i * PIECE, PIECE), pl.ds(2 * MARGIN, MIDDLE.size)],
                mid_send.at[d, i], mid_recv.at[d, i], shifted(dr, 0),
            )
            detour = remote(
                src, relay.at[i], mid_send.at[d, i], relay_recv.at[i], shifted(-dr, 0)
            )
            start_either(middles[dr, i], detour, taken)
    for d, (dr, dc) in enumerate(BESIDE):
        src_c, dst_c = edge_span(dc)
        side = remote(
            field.at[:, :, src_c], framed.at[:, pl.ds(MARGIN, TILE), dst_c],
            side_send.at[d], side_recv.at[d], shifted(dr, dc),
        )
        copies.append(side)
    for copy in copies:
        copy.start()
    own.start()
    own_meta.start()
    for d, dr in enumerate((1, -1)):
        _, rows = edge_span(dr)
        for e, dc in enumerate((-1, 1)):
            ends[dr, e].wait()
            _, lanes = edge_span(dc)
            corner = remote(
                framed.at[:, rows, pl.ds(MARGIN + ENDS[e], MARGIN)], framed.at[:, rows, lanes],
                corner_send.at[d, e], corner_recv.at[d, e], shifted(0, dc),
            )
            corner.start()
            copies.append(corner)
    onward = {}
    for d, dr in enumerate((1, -1)):
        _, handed = relays(dr)
        _, dst_r = edge_span(dr)
        for i in range(2):
            onward[dr, i] = remote(
                relay.at[i],
                framed.at[:, pl.ds(dst_r.start + i * PIECE, PIECE), pl.ds(2 * MARGIN, MIDDLE.size)],
                on_send.at[i], mid_recv.at[d, i], shifted(2 * dr, 0),
            )
            arrived = remote(
                relay.at[i], relay.at[i], on_send.at[i], relay_recv.at[i], shifted(2 * dr, 0)
            )

            @pl.when(handed)
            def _():
                arrived.wait_recv()
                onward[dr, i].start()

    own.wait()
    own_meta.wait()
    for copy in copies:
        copy.wait()
    for copy in middles.values():
        copy.wait()
    for (dr, _), copy in onward.items():
        pl.when(relays(dr)[1])(copy.wait_send)


def gather_frame(field, meta):
    any_spec = pl.BlockSpec(memory_space=pl.ANY)
    count = len(NEIGHBOURS)
    vmem = pl.BlockSpec(memory_space=pltpu.VMEM)
    dma = pltpu.SemaphoreType.DMA
    return pl.pallas_call(
        halo_kernel,
        out_shape=(
            jax.ShapeDtypeStruct((2, EXT, EXT), jnp.float32),
            jax.ShapeDtypeStruct((9, 8, 128), jnp.int32),
        ),
        in_specs=[pl.BlockSpec(memory_space=pltpu.HBM), any_spec],
        out_specs=(vmem, any_spec),
        scratch_shapes=[
            pltpu.VMEM((2, 2, PIECE, MIDDLE.size), jnp.float32),
            dma((2,)), dma((2,)), dma((2,)), dma((2, 2)), dma((2, 2)), dma((2, 2)), dma((2, 2)),
            dma((2,)), dma((2,)), dma((2, 2)), dma((2, 2)), dma((count,)), dma((count,)),
        ],
        compiler_params=pltpu.CompilerParams(
            collective_id=0, has_side_effects=True, vmem_limit_bytes=16 * 1024 * 1024
        ),
        name="halo",
    )(field, meta)


def split(x):
    high = x.astype(jnp.bfloat16)
    return high, (x - high.astype(jnp.float32)).astype(jnp.bfloat16)


def tables():
    n = np.arange(HALF)
    angle = 2.0 * np.pi * ((n[:, None] * n[None, :]) % HALF) / HALF
    cosine, sine = np.cos(angle), np.sin(angle)
    right = np.block([[cosine, -sine], [sine, cosine]]).astype(np.float32)
    half_angle = 2.0 * np.pi * n / EDGE
    twist = np.stack([np.cos(half_angle), np.sin(half_angle)]).astype(np.float32)
    lanes = np.broadcast_to(twist[:, None, :], (2, 8, HALF))
    subs = np.broadcast_to(twist[:, :, None], (2, HALF, HALF))
    order = np.concatenate([np.arange(0, EDGE, 2), np.arange(1, EDGE, 2)])
    pick = (order[:, None] == np.arange(EDGE)[None, :]).astype(np.float32)
    out = []
    for table in (right, right.T):
        high = table.astype(jnp.bfloat16)
        out += [high, (table - high.astype(np.float32)).astype(jnp.bfloat16)]
    out += [pick.astype(jnp.bfloat16), pick.T.astype(jnp.bfloat16)]
    twists = np.concatenate([subs, lanes], 1)
    return [jnp.asarray(np.stack(out)), jnp.asarray(twists)]


def cat(parts, axis):
    return jnp.concatenate(parts, axis=axis)


def tile_kernel(
    place, metas, framed, probe, amps, mats, twists,
    grad, shade, sums,
    patch, xh, xl, yh, yl, amp, light, power, whole, back, far, near, update,
):
    f32, bf16 = jnp.float32, jnp.bfloat16
    dot = functools.partial(jnp.dot, preferred_element_type=f32)
    lane = lax.broadcasted_iota(jnp.int32, (1, HALF), 1)
    top, left = place[0], place[1]
    rh, rl, lh, ll, pick, pick_t = (mats.at[n] for n in range(6))
    sub_tw, lane_tw = twists.at[:, pl.ds(0, HALF), :], twists.at[:, pl.ds(HALF, 8), :]

    grad[...] = jnp.zeros_like(grad)
    sums[...] = jnp.zeros_like(sums)
    for i in range(0, EDGE, ROWS):
        s = pl.ds(i, ROWS)
        power[s, :] = sum(probe[c, k, s, :] * probe[c, k, s, :] for k in range(2) for c in range(2))
    light[pl.ds(256, TILE), pl.ds(256, TILE)] = jnp.zeros((TILE, TILE), f32)

    def spread(low, high, down, shift):
        below = jnp.zeros((8, HALF), f32)
        low, high = (
            pltpu.roll(pltpu.roll(cat([v, below], 0), down, 0), shift, 1) for v in (low, high)
        )
        keep = lane >= shift
        return (
            jnp.where(keep, low, 0.0),
            jnp.where(keep, high, low),
            jnp.where(keep, 0.0, high),
        )

    def light_slot(which, position):
        r = metas[which, 0, position] - top + 256
        c = metas[which, 1, position] - left + 256

        @pl.when((r > 0) & (r < 768) & (c > 0) & (c < 768))
        def _():
            shift, down = lax.rem(c, HALF), lax.rem(r, 8)
            base = pl.multiple_of(c - shift, HALF)
            first = pl.multiple_of(r - down, 8)
            for i in range(0, EDGE, ROWS):
                s = pl.ds(i, ROWS)
                blocks = spread(power[s, :HALF], power[s, HALF:], down, shift)
                for b, block in enumerate(blocks):
                    at = (pl.ds(first + i, ROWS + 8), pl.ds(base + b * HALF, HALF))
                    light[at] += block

    def light_tile(which, _):
        def one(position, _):
            light_slot(which, position)
            return 0

        lax.fori_loop(0, metas[which, 2, 0], one, 0)
        return 0

    lax.fori_loop(0, 9, light_tile, 0)
    for i in range(0, TILE, ROWS):
        shade[pl.ds(i, ROWS), :] = 1.0 / (light[pl.ds(256 + i, ROWS), pl.ds(256, TILE)] + 1.0)

    def visit(position, _):
        r = metas[4, 0, position] - top + MARGIN
        c = metas[4, 1, position] - left + MARGIN
        shift = lax.rem(c, HALF)
        base = pl.multiple_of(c - shift, HALF)
        down = lax.rem(r, 8)
        first = pl.multiple_of(r - down, 8)
        up = lax.rem(ROWS + 8 - down, ROWS + 8)
        back_shift = lax.rem(HALF - shift, HALF)
        keep = lane < HALF - shift
        cosine_l, sine_l = lane_tw[0, :1, :], lane_tw[1, :1, :]

        def block_of(k, part, row=0, rows=EDGE):
            return pl.ds((2 * k + part) * EDGE + row, rows)

        def put(high_ref, low_ref, at, value):
            high, low = split(value)
            high_ref[at] = high
            low_ref[at] = low

        def take_patch():
            for i in range(0, EDGE, ROWS):
                s = pl.ds(i, ROWS)
                for plane in range(2):
                    rolled = [
                        pltpu.roll(
                            pltpu.roll(
                                framed[
                                    plane, pl.ds(first + i, ROWS + 8), pl.ds(base + b * HALF, HALF)
                                ],
                                up,
                                0,
                            )[:ROWS],
                            back_shift,
                            1,
                        )
                        for b in range(3)
                    ]
                    patch[plane, s, :HALF] = jnp.where(keep, rolled[0], rolled[1])
                    patch[plane, s, HALF:] = jnp.where(keep, rolled[1], rolled[2])

        def wave(k):
            for i in range(0, EDGE, ROWS):
                s = pl.ds(i, ROWS)
                wr, wi = [], []
                for h in range(2):
                    cols = pl.ds(h * HALF, HALF)
                    pr, pi = probe[0, k, s, cols], probe[1, k, s, cols]
                    vr, vi = patch[0, s, cols], patch[1, s, cols]
                    wr.append(pr * vr - pi * vi)
                    wi.append(pr * vi + pi * vr)
                dr, di = wr[0] - wr[1], wi[0] - wi[1]
                put(xh, xl, (block_of(k, 0, i, ROWS), slice(None)), cat([wr[0] + wr[1], wi[0] + wi[1]], 1))
                put(
                    xh, xl, (block_of(k, 1, i, ROWS), slice(None)),
                    cat([dr * cosine_l + di * sine_l, di * cosine_l - dr * sine_l], 1),
                )

        def columns(k, high, low, to):
            s = pl.ds(2 * k * EDGE, 2 * EDGE)
            table = cat([high[...], high[...], low[...]], 0)
            to[s, :] = dot(cat([xh[s, :], xl[s, :], xh[s, :]], 1), table)

        def rows(k, part, high, low, to):
            n = 2 * k + part
            table = cat([high[...], high[...], low[...]], 1)
            to[n] = dot(table, cat([yh[n], yl[n], yh[n]], 0))

        def halve_rows(k):
            for i in range(0, HALF, ROWS):
                res = []
                for row in (i, HALF + i):
                    parts = [whole[block_of(k, part, row, ROWS), :] for part in range(2)]
                    res.append(
                        (
                            cat([parts[0][:, :HALF], parts[1][:, :HALF]], 1),
                            cat([parts[0][:, HALF:], parts[1][:, HALF:]], 1),
                        )
                    )
                (tr, ti), (br, bi) = res
                cosine = cat([sub_tw[0, pl.ds(i, ROWS), :]] * 2, 1)
                sine = cat([sub_tw[1, pl.ds(i, ROWS), :]] * 2, 1)
                dr, di = tr - br, ti - bi
                for part, real, imag in (
                    (0, tr + br, ti + bi),
                    (1, dr * cosine + di * sine, di * cosine - dr * sine),
                ):
                    for start, value in ((0, real), (HALF, imag)):
                        put(yh, yl, (2 * k + part, pl.ds(start + i, ROWS), slice(None)), value)

        def scale(part):
            for i in range(0, HALF, ROWS):
                pieces = [
                    (far[2 * k + part, pl.ds(i, ROWS), :], far[2 * k + part, pl.ds(HALF + i, ROWS), :])
                    for k in range(2)
                ]
                total = sum(a * a + b * b for a, b in pieces)
                total = jnp.maximum(total * (1.0 / 65536.0), 0.25)
                factor = amp[pl.ds(part * HALF + i, ROWS), :] * lax.rsqrt(total) - 1.0
                factor = factor * (1.0 / 65536.0)
                for k in range(2):
                    for start, value in ((0, pieces[k][0]), (HALF, pieces[k][1])):
                        at = (2 * k + part, pl.ds(start + i, ROWS), slice(None))
                        put(yh, yl, at, value * factor)

        def join_rows(k):
            for i in range(0, HALF, ROWS):
                (ar, ai), (br, bi) = (
                    (near[2 * k + part, pl.ds(i, ROWS), :], near[2 * k + part, pl.ds(HALF + i, ROWS), :])
                    for part in range(2)
                )
                cosine = cat([sub_tw[0, pl.ds(i, ROWS), :]] * 2, 1)
                sine = cat([sub_tw[1, pl.ds(i, ROWS), :]] * 2, 1)
                br, bi = br * cosine - bi * sine, bi * cosine + br * sine
                for row, real, imag in ((i, ar + br, ai + bi), (HALF + i, ar - br, ai - bi)):
                    for part in range(2):
                        cols = slice(part * HALF, (part + 1) * HALF)
                        put(
                            xh, xl, (block_of(k, part, row, ROWS), slice(None)),
                            cat([real[:, cols], imag[:, cols]], 1),
                        )

        def gather_sums(k):
            for i in range(0, EDGE, ROWS):
                s = pl.ds(i, ROWS)
                parts = [back[block_of(k, part, i, ROWS), :] for part in range(2)]
                ar, ai = parts[0][:, :HALF], parts[0][:, HALF:]
                br, bi = parts[1][:, :HALF], parts[1][:, HALF:]
                br, bi = br * cosine_l - bi * sine_l, bi * cosine_l + br * sine_l
                changed = [[None, None], [None, None]]
                for h, real, imag in ((0, ar + br, ai + bi), (1, ar - br, ai - bi)):
                    cols = pl.ds(h * HALF, HALF)
                    pr, pi = probe[0, k, s, cols], probe[1, k, s, cols]
                    vr, vi = patch[0, s, cols], patch[1, s, cols]
                    ur, ui = pr * real + pi * imag, pr * imag - pi * real
                    sums[k, s, cols] += vr * real + vi * imag
                    sums[2 + k, s, cols] += vr * imag - vi * real
                    if k == 0:
                        update[0, s, cols] = ur
                        update[1, s, cols] = ui
                        sums[4, s, cols] += vr * vr + vi * vi
                    else:
                        changed[0][h] = update[0, s, cols] + ur
                        changed[1][h] = update[1, s, cols] + ui
                if k == 1:
                    for plane in range(2):
                        for b, block in enumerate(spread(*changed[plane], down, shift)):
                            at = (plane, pl.ds(first + i, ROWS + 8), pl.ds(base + b * HALF, HALF))
                            grad[at] += block

        take_patch()
        wave(0)
        columns(0, rh, rl, whole)
        wave(1)
        columns(1, rh, rl, whole)
        picked = dot(pick[...], amps[position]).astype(bf16)
        halve_rows(0)
        rows(0, 0, lh, ll, far)
        rows(0, 1, lh, ll, far)
        amp[...] = dot(picked, pick_t[...])
        halve_rows(1)
        rows(1, 0, lh, ll, far)
        rows(1, 1, lh, ll, far)
        scale(0)
        rows(0, 0, rh, rl, near)
        rows(1, 0, rh, rl, near)
        scale(1)
        rows(0, 1, rh, rl, near)
        rows(1, 1, rh, rl, near)
        join_rows(0)
        columns(0, lh, ll, back)
        join_rows(1)
        columns(1, lh, ll, back)
        gather_sums(0)
        gather_sums(1)
        return 0

    lax.fori_loop(0, metas[4, 2, 0], visit, 0)


def tile_terms(place, metas, framed, probe, amps):
    vmem = pl.BlockSpec(memory_space=pltpu.VMEM)
    smem = pl.BlockSpec(memory_space=pltpu.SMEM)
    f32, bf16 = jnp.float32, jnp.bfloat16
    consts = tables()
    return pl.pallas_call(
        tile_kernel,
        out_shape=(
            jax.ShapeDtypeStruct((2, EXT, EXT), f32),
            jax.ShapeDtypeStruct((TILE, TILE), f32),
            jax.ShapeDtypeStruct((5, EDGE, EDGE), f32),
        ),
        in_specs=[smem, smem] + [vmem] * (3 + len(consts)),
        out_specs=(vmem, vmem, vmem),
        scratch_shapes=[
            pltpu.VMEM((2, EDGE, EDGE), f32),
            pltpu.VMEM((4 * EDGE, EDGE), bf16),
            pltpu.VMEM((4 * EDGE, EDGE), bf16),
            pltpu.VMEM((4, EDGE, EDGE), bf16),
            pltpu.VMEM((4, EDGE, EDGE), bf16),
            pltpu.VMEM((EDGE, EDGE), f32),
            pltpu.VMEM((LIT, LIT_PAD), f32),
            pltpu.VMEM((EDGE, EDGE), f32),
            pltpu.VMEM((4 * EDGE, EDGE), f32),
            pltpu.VMEM((4 * EDGE, EDGE), f32),
            pltpu.VMEM((4, EDGE, EDGE), f32),
            pltpu.VMEM((4, EDGE, EDGE), f32),
            pltpu.VMEM((2, EDGE, EDGE), f32),
        ],
        compiler_params=pltpu.CompilerParams(vmem_limit_bytes=40 * 1024 * 1024),
        name="tile",
    )(place, metas, framed, probe, amps, *consts)


RIM_SOURCE = {-1: (0, MARGIN), 0: (MARGIN, TILE), 1: (MARGIN + TILE, MARGIN)}
CORNERS = (2, 3, 4, 5)
PIECES = tuple(
    piece for i in range(4) for piece in ((0, i), (1, i), (CORNERS[i], 0), (6, i), (7, i))
)
SLOT = (5, 4, 3, 2, 2, 2, 2)
RIM_TARGET = {1: (0, MARGIN), 0: (0, TILE), -1: (TILE - MARGIN, MARGIN)}


def torus_place():
    row, col = lax.axis_index("row"), lax.axis_index("col")
    return (
        row // 8,
        lax.rem(row, 4),
        (col // 2) * 2 + lax.rem(row // 4, 2),
        lax.rem(col, 2),
    )


def torus_device(x, y, z, core):
    return (x * 8 + lax.rem(z, 2) * 4 + y, (z // 2) * 2 + core)


def fold_kernel(
    grad, field, shade, sums, probe, object_out, probe_out,
    base, rims_r, rims_c, rims_d, pair_in, x_in, y_in, z_in, acc, rows_out, row_new, rows_in, spread,
    local_sems, rim_send, rim_recv, red_send, red_recv, put_send, put_recv,
):
    f32 = jnp.float32
    x, y, z, core = torus_place()
    pair = torus_device(x, y, z, 1 - core)
    x_peers = [torus_device(lax.rem(x + d, 4), y, z, core) for d in range(1, 4)]
    y_peers = [torus_device(x, lax.rem(y + d, 4), z, core) for d in range(1, 4)]
    z_peers = [torus_device(x, y, lax.rem(z + d, 8), core) for d in range(1, 8)]

    def ref_of(n):
        if n < 2:
            return rims_c.at[n]
        if n < 6:
            return rims_d.at[n - 2]
        return rims_r.at[n - 6]

    barrier = pltpu.get_barrier_semaphore()
    partners = [shifted(dr, dc) for dr, dc in NEIGHBOURS] + [pair] + x_peers + y_peers + z_peers
    for device in partners:
        pl.semaphore_signal(barrier, inc=1, device_id=device, device_id_type=MESH)
    locals_ = [
        pltpu.make_async_copy(field, base, local_sems.at[0]),
    ]
    pl.semaphore_wait(barrier, len(partners))

    def send(src, dst, device, sems, n):
        copy = pltpu.make_async_remote_copy(
            src_ref=src,
            dst_ref=dst,
            send_sem=sems[0].at[n],
            recv_sem=sems[1].at[n],
            device_id=device,
            device_id_type=MESH,
        )
        copy.start()
        return copy

    red, put = (red_send, red_recv), (put_send, put_recv)
    half = pl.multiple_of(core * HALF, HALF)
    other = pl.multiple_of((1 - core) * HALF, HALF)
    to_pair = send(sums.at[:, pl.ds(other, HALF), :], pair_in, pair, red, 0)
    rims = []

    def send_rims(count):
        for n, i in PIECES[len(rims) : len(rims) + count]:
            dr, dc = NEIGHBOURS[n]
            (r0, rn), (c0, cn) = RIM_SOURCE[dr], RIM_SOURCE[dc]
            size = rn if n in CORNERS else rn // 4
            src = grad.at[:, pl.ds(r0 + i * size, size), pl.ds(c0, cn)]
            dst = ref_of(n).at[:, pl.ds(i * size, size), :]
            rims.append(send(src, dst, shifted(dr, dc), (rim_send, rim_recv), len(rims)))

    send_rims(SLOT[0])
    for copy in locals_:
        copy.start()

    to_pair.wait()
    for i in range(0, HALF, ROWS):
        rows = pl.ds(i, ROWS)
        acc[:, rows, :] = sums[:, pl.ds(pl.multiple_of(half + i, ROWS), ROWS), :] + pair_in[:, rows, :]
    turns = ((x, x_peers, y, y_peers), (y, y_peers, x, x_peers))
    copies = []
    for d in range(1, 4):
        for h, (one, one_peers, _, _) in enumerate(turns):
            at = pl.multiple_of(lax.rem(one + d, 4) * 32, 32)
            src = acc.at[:, pl.ds(at, 32), pl.ds(h * HALF, HALF)]
            copies.append(send(src, x_in.at[h, d - 1], one_peers[d - 1], red, 3 * h + d))
    send_rims(SLOT[1])
    for copy in copies:
        copy.wait()
    copies = []
    ats = []
    for h, (one, _, two, two_peers) in enumerate(turns):
        lanes = pl.ds(h * HALF, HALF)
        at = pl.multiple_of(one * 32, 32)
        mine = acc[:, pl.ds(at, 32), lanes]
        for d in range(3):
            mine = mine + x_in[h, d]
        acc[:, pl.ds(at, 32), lanes] = mine
        ats.append((at, pl.multiple_of(at + two * 8, 8)))
        for d in range(1, 4):
            to = pl.multiple_of(at + lax.rem(two + d, 4) * 8, 8)
            src = acc.at[:, pl.ds(to, 8), lanes]
            copies.append(send(src, y_in.at[h, d - 1], two_peers[d - 1], red, 6 + 3 * h + d))
    send_rims(SLOT[2])
    for copy in copies:
        copy.wait()
    halves = []
    for h in range(2):
        part = acc[:, pl.ds(ats[h][1], 8), pl.ds(h * HALF, HALF)]
        for d in range(3):
            part = part + y_in[h, d]
        halves.append(part)
    mine = jnp.concatenate(halves, 2)
    rows_out[...] = jnp.swapaxes(jnp.concatenate([mine, jnp.zeros((3, 8, EDGE), f32)], 0), 0, 1)
    copies = []
    for d in range(1, 8):
        copies.append(send(rows_out.at[lax.rem(z + d, 8)], z_in.at[d - 1], z_peers[d - 1], red, 12 + d))
    send_rims(SLOT[3])
    for copy in copies:
        copy.wait()
    total = rows_out[z]
    for d in range(7):
        total = total + z_in[d]
    row_new[...] = total / (total[4:5] + 1.0)

    copies = []
    for d in range(1, 8):
        copies.append(send(row_new, rows_in.at[z], z_peers[d - 1], put, d))
    rows_in[z] = row_new[...]
    send_rims(SLOT[4])
    for copy in copies:
        copy.wait()
    planes = jnp.swapaxes(rows_in[...], 0, 1)[:4]
    copies = []
    for h in range(2):
        at, lanes = pl.multiple_of(half + ats[h][1], 8), pl.ds(h * HALF, HALF)
        spread[:, pl.ds(at, 8), lanes] = planes[:, :, h * HALF : (h + 1) * HALF]
        block = spread.at[:, pl.ds(at, 8), lanes]
        for d in range(1, 4):
            copies.append(send(block, block, turns[h][3][d - 1], put, 7 + 3 * h + d))
    send_rims(SLOT[5])
    for copy in copies:
        copy.wait()
    copies = []
    for d in range(1, 4):
        for h in range(2):
            at = pl.multiple_of(half + ats[h][0], 32)
            block = spread.at[:, pl.ds(at, 32), pl.ds(h * HALF, HALF)]
            copies.append(send(block, block, turns[h][1][d - 1], put, 13 + 3 * h + d))
    send_rims(SLOT[6])
    for copy in locals_:
        copy.wait()
    for i in range(0, TILE, ROWS):
        rows = pl.ds(i, ROWS)
        for c in range(2):
            object_out[c, rows, :] = (
                base[c, rows, :]
                + grad[c, pl.ds(MARGIN + i, ROWS), pl.ds(MARGIN, TILE)] * shade[rows, :]
            )
    for copy in copies:
        copy.wait()
    block = spread.at[:, pl.ds(half, HALF), :]
    last = send(block, block, pair, put, 0)

    for copy in rims:
        copy.wait()
    for n, (dr, dc) in enumerate(NEIGHBOURS):
        (r0, rn), (c0, cn) = RIM_TARGET[dr], RIM_TARGET[dc]
        for i in range(0, rn, 64):
            rows = pl.ds(r0 + i, 64)
            object_out[:, rows, pl.ds(c0, cn)] += ref_of(n)[:, pl.ds(i, 64), :] * shade[rows, pl.ds(c0, cn)]
    last.wait()
    for c in range(2):
        for k in range(2):
            probe_out[c, k] = probe[c, k] + spread[2 * c + k]


def fold(grad, field, shade, sums, probe):
    vmem = pl.BlockSpec(memory_space=pltpu.VMEM)
    any_spec = pl.BlockSpec(memory_space=pl.ANY)
    f32 = jnp.float32
    dma = pltpu.SemaphoreType.DMA
    return pl.pallas_call(
        fold_kernel,
        out_shape=(
            jax.ShapeDtypeStruct((2, TILE, TILE), f32),
            jax.ShapeDtypeStruct((2, 2, EDGE, EDGE), f32),
        ),
        in_specs=[vmem, any_spec, vmem, vmem, vmem],
        out_specs=(vmem, vmem),
        scratch_shapes=[
            pltpu.VMEM((2, TILE, TILE), f32),
            pltpu.VMEM((2, 2, MARGIN, TILE), f32),
            pltpu.VMEM((2, 2, TILE, MARGIN), f32),
            pltpu.VMEM((4, 2, MARGIN, MARGIN), f32),
            pltpu.VMEM((5, HALF, EDGE), f32),
            pltpu.VMEM((2, 3, 5, 32, HALF), f32),
            pltpu.VMEM((2, 3, 5, 8, HALF), f32),
            pltpu.VMEM((7, 8, EDGE), f32),
            pltpu.VMEM((5, HALF, EDGE), f32),
            pltpu.VMEM((8, 8, EDGE), f32),
            pltpu.VMEM((8, EDGE), f32),
            pltpu.VMEM((8, 8, EDGE), f32),
            pltpu.VMEM((4, EDGE, EDGE), f32),
            dma((1,)), dma((len(PIECES),)), dma((len(PIECES),)), dma((20,)), dma((20,)), dma((20,)), dma((20,)),
        ],
        compiler_params=pltpu.CompilerParams(
            collective_id=1, has_side_effects=True, vmem_limit_bytes=32 * 1024 * 1024
        ),
        name="fold",
    )(grad, field, shade, sums, probe)


def on_device(field, probe, offsets, counts, amps):
    row, col = lax.axis_index("row"), lax.axis_index("col")
    meta = jnp.pad(offsets[0, 0], ((0, 6), (0, 128 - SLOTS))) + jnp.pad(counts, ((2, 5), (0, 127)))
    framed, metas = gather_frame(field, meta)
    place = jnp.stack([row * TILE, col * TILE]).astype(jnp.int32)
    grad, shade, sums = tile_terms(place, metas, framed, probe, amps[0, 0])
    return fold(grad, field, shade, sums, probe)


def solution(mesh):
    in_specs = (
        P(None, "row", "col"),
        P(),
        P("row", "col", None, None),
        P("row", "col"),
        P("row", "col", None, None, None),
    )
    out_specs = (P(None, "row", "col"), P())
    return jax.shard_map(
        on_device, mesh=mesh, in_specs=in_specs, out_specs=out_specs, check_vma=False
    )
```
